256 devices in a mesh: dom: 128 (over x, z, y), mp: 2 (over core).
Axes of the slice: x: 4, y: 4, z: 8, core: 2. Of those that a mesh axis runs over, the one named last changes fastest.
Arguments:
- node_feats: bfloat16 [32768, 1024], P('dom'), may hold values from -24 to 24
- proj_weight: bfloat16 [1024, 3, 1024], P(None, None, 'mp'), may hold values from -0.1875 to 0.1875
- norm_gain: float32 [2, 1024], P(None, 'mp'), may hold values from 0.25 to 1.75
- grad_out: bfloat16 [32768, 1024], P('dom', 'mp'), may hold values from -6 to 6
- tile_lists: int32 [256, 6], P('dom'), may hold values from 0 to 9, as said below
- tile_valid: int32 [256], P('dom'), may hold values from 1 to 128, as said below
- send_rows: int32 [16384, 8], P('dom'), may hold values from 0 to 255
- send_count: int32 [128, 128], P('dom'), may hold values from 1 to 8, as said below
Outputs:
- proj_grad: float32 [1024, 3, 1024], P('dom', None, 'mp')
- input_grad: bfloat16 [32768, 1024], P('dom', 'mp')
The draws below stay inside these ranges and needn't reach their ends.
Inputs may be any that keep to these rules, and one draw needn't show every extreme that they name: `tile_lists`: entries below 2 name the partition's own tiles, the others name tiles of its received slots. `tile_valid`: at least one tile is full. `send_rows`: local row numbers in the sending partition; slots at or beyond the count are unused. `send_count`: row p, column d: the used slots from partition p to partition d; every partition fills all 8 slots to some peer.
All inputs are finite; a program needn't handle non-finite values.
Results may differ from the reference program's by a relative error of at most 0.015.
Values may be sent and summed in bfloat16 or wider, within the bound.
A program may use at most 128 MiB of HBM per device.

```python
import math
import jax
import jax.numpy as jnp
from jax import lax

D = 1024
H = 16
TILE = 128
NT_DEV = 2
EL = 2
ER = 4
RT = 8
CAP = 8
ROWS_DEV = 256
N_TILES = 256
NODES = 32768
N_DOM = 128


def draw_tile_lists(key, part):
    key = jax.random.fold_in(key, 11)
    own_key, far_key = jax.random.split(key)
    own_scores = jax.random.randint(own_key, (N_TILES, NT_DEV), 0, 1 << 16) * NT_DEV + jnp.arange(NT_DEV, dtype=jnp.int32)[None, :]
    far_scores = jax.random.randint(far_key, (N_TILES, RT), 0, 1 << 16) * RT + jnp.arange(RT, dtype=jnp.int32)[None, :]
    own_pick = jnp.argsort(own_scores, axis=1, stable=True)[:, :EL]
    far_pick = jnp.argsort(far_scores, axis=1, stable=True)[:, :ER] + NT_DEV
    return jnp.concatenate([own_pick, far_pick], axis=1).astype(jnp.int32)


def draw_tile_valid(key, part):
    key = jax.random.fold_in(key, 23)
    value_key, full_key = jax.random.split(key)
    counts = jax.random.randint(value_key, (N_TILES,), 1, TILE + 1)
    full_tile = jax.random.randint(full_key, (), 0, N_TILES)
    places = jnp.arange(N_TILES, dtype=jnp.int32)
    return jnp.where(places == full_tile, TILE, counts).astype(jnp.int32)


def draw_send_count(key, part):
    key = jax.random.fold_in(key, 37)
    count_key, full_key, hub_key = jax.random.split(key, 3)
    counts = jax.random.randint(count_key, (N_DOM, N_DOM), 1, CAP + 1)
    full_peer = jax.random.randint(full_key, (N_DOM,), 0, N_DOM)
    hub_owner = jax.random.randint(hub_key, (N_DOM,), 0, 4) == 0
    peers = jnp.arange(N_DOM, dtype=jnp.int32)[None, :]
    filled = (peers == full_peer[:, None]) | hub_owner[:, None]
    return jnp.where(filled, CAP, counts).astype(jnp.int32)


def plant(entries, stream_key, smallest, high):
    longest = entries.shape.index(max(entries.shape))
    spots = []
    for shift in (0, 1):
        where = [jax.random.randint(jax.random.fold_in(stream_key, axis), (), 0, length) for axis, length in enumerate(entries.shape)]
        where[longest] = (where[longest] + shift) % entries.shape[longest]
        spots.append(tuple(where))
    return entries.at[spots[0]].set(smallest).at[spots[1]].set(high)


def with_spikes(array, stream_key, source, target, blocks, factor):
    owner, partner = [(jnp.arange(array.shape[axis_at]) // (array.shape[axis_at] // blocks)).reshape([-1 if axis == axis_at else 1 for axis in range(array.ndim)]) for axis_at in (source, target)]
    chosen = jax.random.permutation(stream_key, blocks)[partner]
    strong = (owner == chosen) | (owner == (partner + blocks // 2) % blocks)
    return jnp.where(strong, factor * array, array)


def steps_of(rng, shape, pieces, smallest, high):
    level, own = 1.0, jax.random.fold_in(rng, 6)
    for dim, blocks in pieces:
        steps = jnp.exp(jax.random.uniform(jax.random.fold_in(own, dim), (blocks,), jnp.float32, smallest / len(pieces), high / len(pieces)))
        level = level * jnp.repeat(steps, shape[dim] // blocks).reshape([-1 if axis == dim else 1 for axis in range(len(shape))])
    return level


def normal_values(stream_key, dims, deviation, reach, pieces=(), kind=jnp.bfloat16):
    array = jax.random.normal(stream_key, dims, jnp.float32) * deviation
    if len(pieces) > 0:
        array = steps_of(stream_key, dims, pieces, -0.22, 0.18) * array
    return jnp.clip(array, min=-reach, max=reach).astype(kind)


def noise_with(rng, dims, deviation, bound, cuts, heavy, held_as=jnp.bfloat16):
    drawn = deviation * jax.random.normal(rng, dims, jnp.float32)
    if cuts:
        drawn = drawn * steps_of(rng, dims, cuts, -0.22, 0.18)
    return jnp.clip(with_spikes(drawn, jax.random.fold_in(rng, 3), *heavy), -bound, bound).astype(held_as)


def setup_inputs(seed: int = 0) -> dict:
    splits = jax.random.split(jax.random.key(seed), 9)
    node_feats = noise_with(splits[0], (NODES, D), 1.0, 24.0, ((0, 128),), (0, 1, 128, 5.5))
    proj_weight = normal_values(splits[1], (D, 3, D), D ** -0.5, 0.1875, ((2, 2),))
    norm_gain = jnp.clip(1.0 + 0.15 * jax.random.normal(splits[2], (2, D), jnp.float32), 0.25, 1.75)
    grad_out = normal_values(splits[3], (NODES, D), 1.0, 6.0, ((0, 128), (1, 2)))
    tile_lists = draw_tile_lists(jax.random.fold_in(splits[8], 71), 0)
    tile_valid = draw_tile_valid(jax.random.fold_in(splits[8], 71), 0)
    send_rows = plant(jax.random.randint(splits[6], (N_DOM * N_DOM, CAP), 0, ROWS_DEV), jax.random.fold_in(splits[6], 1), 0, ROWS_DEV - 1).astype(jnp.int32)
    send_count = draw_send_count(jax.random.fold_in(splits[8], 71), 0)
    return {"node_feats": node_feats, "proj_weight": proj_weight, "norm_gain": norm_gain, "grad_out": grad_out, "tile_lists": tile_lists, "tile_valid": tile_valid, "send_rows": send_rows, "send_count": send_count}


norm_eps = 1e-06

def rms_heads(raw_rows, gain_row, head_count):
    row_count, col_width = raw_rows.shape
    shaped = raw_rows.reshape(row_count, head_count, col_width // head_count)
    inverse = lax.rsqrt(lax.optimization_barrier(jnp.mean(shaped * shaped, axis=2, keepdims=True)) + norm_eps)
    return ((shaped * inverse).reshape(row_count, col_width) * gain_row, inverse)

def rms_back(raw_rows, inverse, gain_row, upstream, head_count):
    row_count, col_width = raw_rows.shape
    shaped = raw_rows.reshape(row_count, head_count, col_width // head_count)
    scaled = (upstream * gain_row).reshape(row_count, head_count, col_width // head_count)
    inner_mean = lax.optimization_barrier(jnp.mean(shaped * scaled, axis=2, keepdims=True))
    result = inverse * scaled - shaped * (inverse * inverse * inverse) * inner_mean
    return result.reshape(row_count, col_width)

def project(node_feats, proj_weight, norm_gain, head_count):
    row_count = node_feats.shape[0]
    col_width = proj_weight.shape[2]
    flat_weight = proj_weight.reshape(proj_weight.shape[0], 3 * col_width)
    mixed_proj = jnp.dot(node_feats, flat_weight, preferred_element_type=jnp.float32).reshape(row_count, 3, col_width)
    q_hat, q_inverse = rms_heads(mixed_proj[:, 0], norm_gain[0], head_count)
    k_hat, k_inverse = rms_heads(mixed_proj[:, 1], norm_gain[1], head_count)
    return (q_hat.astype(jnp.bfloat16), k_hat.astype(jnp.bfloat16), mixed_proj[:, 2].astype(jnp.bfloat16), mixed_proj, q_inverse, k_inverse)

def attend_back(q_hat, k_table, v_table, key_live, tile_lists, upstream, head_count):
    tile_count, list_len = tile_lists.shape
    table_tiles = k_table.shape[0] // TILE
    col_width = q_hat.shape[1]
    head_dim = col_width // head_count
    score_scale = 1.0 / math.sqrt(head_dim)
    flat_lists = tile_lists.reshape(-1)
    key_rows = k_table.reshape(table_tiles, TILE, col_width)[flat_lists]
    key_rows = key_rows.reshape(tile_count, list_len * TILE, head_count, head_dim).astype(jnp.float32)
    value_rows = v_table.reshape(table_tiles, TILE, col_width)[flat_lists]
    value_rows = value_rows.reshape(tile_count, list_len * TILE, head_count, head_dim).astype(jnp.float32)
    live_rows = key_live.reshape(table_tiles, TILE)[flat_lists].reshape(tile_count, 1, 1, list_len * TILE)
    queries = q_hat.reshape(tile_count, TILE, head_count, head_dim).astype(jnp.float32)
    grad_rows = upstream.reshape(tile_count, TILE, head_count, head_dim).astype(jnp.float32)
    scores = jnp.einsum('tqhd,tkhd->thqk', queries, key_rows) * score_scale
    weights = jnp.where(live_rows, jnp.exp(scores), jnp.zeros_like(scores))
    prob_full = weights / lax.optimization_barrier(jnp.sum(weights, axis=3, keepdims=True))
    prob_low = lax.optimization_barrier(prob_full.astype(jnp.bfloat16)).astype(jnp.float32)
    output = jnp.einsum('thqk,tkhd->tqhd', prob_low, value_rows)
    row_delta = lax.optimization_barrier(jnp.sum(grad_rows * output, axis=3))
    grad_values = jnp.einsum('thqk,tqhd->tkhd', prob_low, grad_rows)
    grad_probs = jnp.einsum('tqhd,tkhd->thqk', grad_rows, value_rows)
    grad_scores = prob_full * (grad_probs - jnp.transpose(row_delta, (0, 2, 1))[:, :, :, None])
    grad_scores = lax.optimization_barrier(grad_scores.astype(jnp.bfloat16)).astype(jnp.float32)
    grad_queries = jnp.einsum('thqk,tkhd->tqhd', grad_scores, key_rows) * score_scale
    grad_keys = jnp.einsum('thqk,tqhd->tkhd', grad_scores, queries) * score_scale
    flat_width = TILE * col_width
    zero_table = jnp.zeros((table_tiles, flat_width), jnp.float32)
    key_table_grad = zero_table.at[flat_lists].add(grad_keys.reshape(tile_count * list_len, flat_width))
    value_table_grad = zero_table.at[flat_lists].add(grad_values.reshape(tile_count * list_len, flat_width))
    return (grad_queries.reshape(tile_count * TILE, col_width), key_table_grad.reshape(table_tiles * TILE, col_width), value_table_grad.reshape(table_tiles * TILE, col_width))

def reference(node_feats, proj_weight, norm_gain, grad_out, tile_lists, tile_valid, send_rows, send_count):
    rows_dev = NT_DEV * TILE
    total_rows, model_width = node_feats.shape
    q_hat, k_hat, values, mixed_proj, q_inverse, k_inverse = project(node_feats, proj_weight, norm_gain, H)
    send_table = send_rows.reshape(N_DOM, N_DOM, CAP)
    peer_base = jnp.arange(N_DOM, dtype=jnp.int32)[:, None] * rows_dev
    tile_pos = jnp.arange(TILE, dtype=jnp.int32)
    slot_pos = jnp.arange(CAP, dtype=jnp.int32)

    def one_part(running, portion):
        key_all, value_all = running
        row_start = (portion * rows_dev).astype(jnp.int32)
        q_part = lax.dynamic_slice_in_dim(q_hat, row_start, rows_dev, 0)
        k_part = lax.dynamic_slice_in_dim(k_hat, row_start, rows_dev, 0)
        v_part = lax.dynamic_slice_in_dim(values, row_start, rows_dev, 0)
        g_part = lax.dynamic_slice_in_dim(grad_out, row_start, rows_dev, 0)
        lists_part = lax.dynamic_slice_in_dim(tile_lists, (portion * NT_DEV).astype(jnp.int32), NT_DEV, 0)
        valid_part = lax.dynamic_slice_in_dim(tile_valid, (portion * NT_DEV).astype(jnp.int32), NT_DEV, 0)
        own_live = (tile_pos[None, :] < valid_part[:, None]).reshape(-1)
        global_rows = (peer_base + send_table[:, portion, :]).reshape(-1)
        slot_live = (slot_pos[None, :] < send_count[:, portion][:, None]).reshape(-1)
        k_table = jnp.concatenate([k_part, k_hat[global_rows]], axis=0)
        v_table = jnp.concatenate([v_part, values[global_rows]], axis=0)
        key_live = jnp.concatenate([own_live, slot_live], axis=0)
        query_grad, key_grad, value_grad = attend_back(q_part, k_table, v_table, key_live, lists_part, g_part, H)
        own_keys = lax.dynamic_slice_in_dim(key_all, row_start, rows_dev, 0) + key_grad[:rows_dev]
        own_values = lax.dynamic_slice_in_dim(value_all, row_start, rows_dev, 0) + value_grad[:rows_dev]
        key_all = lax.dynamic_update_slice_in_dim(key_all, own_keys, row_start, 0)
        value_all = lax.dynamic_update_slice_in_dim(value_all, own_values, row_start, 0)
        key_all = key_all.at[global_rows].add(key_grad[rows_dev:])
        value_all = value_all.at[global_rows].add(value_grad[rows_dev:])
        return ((key_all, value_all), query_grad)
    zero_rows = jnp.zeros((total_rows, model_width), jnp.float32)
    (key_all, value_all), query_parts = lax.scan(one_part, (zero_rows, zero_rows), jnp.arange(N_DOM, dtype=jnp.int32))
    query_hat_grad = query_parts.reshape(total_rows, model_width)
    query_grad = rms_back(mixed_proj[:, 0], q_inverse, norm_gain[0], query_hat_grad, H)
    key_grad = rms_back(mixed_proj[:, 1], k_inverse, norm_gain[1], key_all, H)
    grads_low = jnp.stack([query_grad, key_grad, value_all], axis=1).astype(jnp.bfloat16)
    grads_low = grads_low.reshape(total_rows, 3 * model_width)
    flat_weight = proj_weight.reshape(model_width, 3 * model_width)
    proj_grad = jnp.dot(node_feats.T, grads_low, preferred_element_type=jnp.float32).reshape(model_width, 3, model_width)
    input_grad = jnp.dot(grads_low, flat_weight.T, preferred_element_type=jnp.float32).astype(jnp.bfloat16)
    return (proj_grad, input_grad)
```

```python
import math

import jax
import jax.numpy as jnp
from jax import lax
from jax.experimental import pallas as pl
from jax.experimental.pallas import tpu as pltpu
from jax.sharding import PartitionSpec as P

DH = 64
TILE = 128
CAP = 8
SLAB = 2 * CAP
EPS = 1e-06
AX, AZ, AY = 4, 8, 4
N = AX * AZ * AY
DEAD = 1024.0
LIVE_MAX = 512.0
LOG2E = math.log2(math.e)
MESH = pl.DeviceIdType.MESH
F32 = jnp.float32
BF16 = jnp.bfloat16


def dot(a, b):
    return jnp.dot(a, b, preferred_element_type=F32)


def dot_nt(a, b):
    return lax.dot_general(a, b, (((1,), (1,)), ((), ())), preferred_element_type=F32)


def dot_tn(a, b):
    return lax.dot_general(a, b, (((0,), (0,)), ((), ())), preferred_element_type=F32)


def place():
    dom = lax.axis_index("dom")
    core = lax.axis_index("mp")
    return dom, core, dom // (AZ * AY), lax.rem(dom // AY, AZ), lax.rem(dom, AY)


def rows_at(start, size):
    return pl.ds(pl.multiple_of(start, SLAB), size)


def greet_all(dom, core):
    barrier = pltpu.get_barrier_semaphore()

    def greet(i, carry):
        peer = lax.rem(dom + 1 + i, N)
        pl.semaphore_signal(barrier, inc=1, device_id={"dom": peer}, device_id_type=MESH)
        return carry

    lax.fori_loop(0, N - 1, greet, 0)
    pl.semaphore_signal(barrier, inc=1, device_id={"mp": 1 - core}, device_id_type=MESH)
    return barrier


def wait_bytes(ref, sem):
    pltpu.make_async_copy(ref, ref, sem).wait()


def push_block(step, mine, src, dst, send_sem, recv_sem):
    dom, core, x, z, y = mine
    far = lax.rem(x + step, AX)

    def push(i, carry):
        dz, dy = i // AY, lax.rem(i, AY)
        peer = far * (AZ * AY) + lax.rem(z + dz, AZ) * AY + lax.rem(y + dy, AY)
        pltpu.make_async_remote_copy(
            src_ref=src.at[rows_at(peer * SLAB, SLAB)],
            dst_ref=dst.at[rows_at(dom * SLAB, SLAB)],
            send_sem=send_sem,
            recv_sem=recv_sem.at[step],
            device_id={"dom": peer},
            device_id_type=MESH,
        ).start()
        return carry

    lax.fori_loop(1 if step == 0 else 0, AZ * AY, push, 0)


BLOCK = AZ * AY * SLAB
BLOCK_KEYS = AZ * AY * CAP


def fetch_kernel(
    idx_ref, feats_ref, table_ref, halves, outgoing, landed, send_sem, recv_sem, pair_send, pair_recv
):
    mine = place()
    dom, core, x, z, y = mine
    barrier = greet_all(dom, core)
    rows, width = feats_ref.shape
    half = width // 2
    quarter = half // 2
    halves[0:rows, :] = feats_ref[:, pl.ds(pl.multiple_of(core * half, half), quarter)]
    halves[rows : 2 * rows, :] = feats_ref[
        :, pl.ds(pl.multiple_of(core * half + quarter, quarter), quarter)
    ]
    halves[2 * rows :, :] = jnp.full((SLAB, quarter), DEAD, BF16)
    for step in range(AX):
        far = lax.rem(x + step, AX)
        wanted = idx_ref[far]
        kinds = lax.broadcasted_iota(jnp.int32, (2 * rows + SLAB, BLOCK), 0)
        pick = jnp.where(kinds == wanted, 1.0, 0.0).astype(BF16)
        outgoing[rows_at(far * BLOCK, BLOCK), :] = dot_tn(pick, halves[...]).astype(BF16)
        if step == 0:
            pl.semaphore_wait(barrier, N)
        push_block(step, mine, outgoing, landed.at[core], send_sem, recv_sem)
    own = rows_at(dom * SLAB, SLAB)
    landed[core, own, :] = outgoing[own, :]
    pairs = []
    for step in range(AX):
        near = lax.rem(x - step + AX, AX)
        part = landed.at[core, rows_at(near * BLOCK, BLOCK)]
        if step == 0:
            wait_bytes(landed.at[core, pl.ds(0, BLOCK - SLAB)], recv_sem.at[step])
        else:
            wait_bytes(part, recv_sem.at[step])
        pair = pltpu.make_async_remote_copy(
            src_ref=part,
            dst_ref=part,
            send_sem=pair_send.at[step],
            recv_sem=pair_recv.at[step],
            device_id={"mp": 1 - core},
            device_id_type=MESH,
        )
        pair.start()
        pairs.append(pair)
    for step in range(AX):
        near = lax.rem(x - step + AX, AX)
        pairs[step].wait()
        keys = rows_at(near * BLOCK_KEYS, BLOCK_KEYS)
        for plane in range(2):
            slabs = landed[plane, rows_at(near * BLOCK, BLOCK), :].astype(F32)
            slabs = slabs.reshape(AZ * AY, SLAB, quarter)
            for side in range(2):
                columns = pl.ds(plane * half + side * quarter, quarter)
                block = slabs[:, side * CAP : (side + 1) * CAP, :].reshape(BLOCK_KEYS, quarter)
                table_ref[keys, columns] = block.astype(BF16)
    sent = outgoing.at[pl.ds(0, (N - 1) * SLAB)]
    wait_bytes(sent, send_sem)


def fetch(idx, feats):
    rows, width = feats.shape
    quarter = width // 4
    return pl.pallas_call(
        fetch_kernel,
        out_shape=jax.ShapeDtypeStruct((N * CAP, width), BF16),
        in_specs=[pl.BlockSpec(memory_space=pltpu.VMEM)] * 2,
        out_specs=pl.BlockSpec(memory_space=pltpu.VMEM),
        scratch_shapes=[
            pltpu.VMEM((2 * rows + SLAB, quarter), BF16),
            pltpu.VMEM((N * SLAB, quarter), BF16),
            pltpu.VMEM((2, N * SLAB, quarter), BF16),
            pltpu.SemaphoreType.DMA,
            pltpu.SemaphoreType.DMA((AX,)),
            pltpu.SemaphoreType.DMA((AX,)),
            pltpu.SemaphoreType.DMA((AX,)),
        ],
        compiler_params=pltpu.CompilerParams(
            collective_id=0, has_side_effects=True, vmem_limit_bytes=40 * 1024 * 1024
        ),
        name="fetch",
    )(idx, feats)


def slabbed(block, width):
    count = block.shape[0] // CAP
    left = block[:, :width].reshape(count, CAP, width)
    right = block[:, width:].reshape(count, CAP, width)
    return jnp.concatenate([left, right], axis=1).reshape(count * SLAB, width)


def layer_kernel(
    lists_ref,
    valid_ref,
    feats_ref,
    table_ref,
    weight_ref,
    gain_ref,
    grad_ref,
    first_ref,
    second_ref,
    keep_ref,
    send_ref,
    feats_t,
    k_hat,
    k_hat_t,
    k_unit,
    k_inv,
    values,
    q_unit,
    q_inv,
    q_t,
    g_t,
    mask_t,
    expo,
    expo_dp,
    dq_t,
    dk_sum,
    dv_sum,
    dk_low,
    dv_low,
):
    core = lax.axis_index("mp")
    rows, width = feats_ref.shape
    cols = grad_ref.shape[1]
    keys = k_hat.shape[0]
    blocks = keys // rows
    pairs = cols // (2 * DH)

    def feats_block(b):
        if b == 0:
            return feats_ref[...]
        return table_ref[(b - 1) * rows : b * rows, :]

    head_of = lax.broadcasted_iota(jnp.int32, (cols, cols), 0) // DH
    head_to = lax.broadcasted_iota(jnp.int32, (cols, cols), 1) // DH
    head_mean = jnp.where(head_of == head_to, 1.0 / DH, 0.0).astype(BF16)

    mixed_q = dot(feats_ref[...], weight_ref[0])
    inv = lax.rsqrt(dot((mixed_q * mixed_q).astype(BF16), head_mean) + EPS)
    unit = mixed_q * inv
    q_inv[...] = inv
    q_unit[...] = unit
    q_scaled = unit * (gain_ref[0:1, :] * (LOG2E / math.sqrt(DH)))
    q_t[...] = q_scaled.T
    g_t[...] = grad_ref[...].astype(F32).T

    for b in range(blocks):
        part = pl.ds(b * rows, rows)
        block = feats_block(b)
        feats_t[:, part] = block.T
        mixed_k = dot(block, weight_ref[1])
        inv = lax.rsqrt(dot((mixed_k * mixed_k).astype(BF16), head_mean) + EPS)
        unit = mixed_k * inv
        k_inv[part, :] = inv
        k_unit[part, :] = unit
        low = (unit * gain_ref[1:2, :]).astype(BF16)
        k_hat[part, :] = low
        k_hat_t[:, part] = low.T
        values[part, :] = dot(block, weight_ref[2]).astype(BF16)

    place_in_tile = lax.broadcasted_iota(jnp.int32, (TILE, TILE), 0)
    for j in range(keys // TILE):
        if j < rows // TILE:
            live = jnp.where(place_in_tile < valid_ref[j], 1.0, 0.0)
        else:
            at = (j - rows // TILE) * TILE
            mark = table_ref[at : at + TILE, 0:TILE].astype(F32)[:, 0:1]
            live = jnp.where(jnp.broadcast_to(mark, (TILE, TILE)) < LIVE_MAX, 1.0, 0.0)
        for t in range(rows // TILE):
            listed = jnp.int32(0)
            for i in range(lists_ref.shape[1]):
                listed += jnp.where(lists_ref[t, i] == j, 1, 0)
            mask_t[j * TILE : (j + 1) * TILE, t * TILE : (t + 1) * TILE] = live * listed.astype(F32)

    which = lax.broadcasted_iota(jnp.int32, (2 * DH, rows), 0) // DH

    def head_pair(pair, carry):
        lanes = pl.ds(pl.multiple_of(pair * 2 * DH, 2 * DH), 2 * DH)
        q_pair = q_t[lanes, :]
        g_pair = g_t[lanes, :]
        for h in range(2):
            q_h = jnp.where(which == h, q_pair, 0.0)
            g_h = jnp.where(which == h, g_pair, 0.0)
            q_low = q_h.astype(BF16)
            g_low = g_h.astype(BF16)
            total = jnp.zeros((1, rows), F32)
            moment = jnp.zeros((1, rows), F32)
            for b in range(blocks):
                part = pl.ds(b * rows, rows)
                e = jnp.exp2(dot(k_hat[part, lanes], q_low)) * mask_t[part, :]
                e_dp = e * dot(values[part, lanes], g_low)
                total += jnp.sum(e, axis=0, keepdims=True)
                moment += jnp.sum(e_dp, axis=0, keepdims=True)
                expo[h, part, :] = e
                expo_dp[h, part, :] = e_dp
            over = 1.0 / total
            delta = moment * over
            q_over = (q_h * (over * (1.0 / LOG2E))).astype(BF16)
            g_over = (g_h * over).astype(BF16)
            dq_h = jnp.zeros((DH, rows), F32)
            head_rows = pl.ds(pl.multiple_of(pair * 2 * DH + h * DH, DH), DH)
            for b in range(blocks):
                part = pl.ds(b * rows, rows)
                e = expo[h, part, :]
                ds = (expo_dp[h, part, :] - e * delta).astype(BF16)
                dv = dot_nt(e.astype(BF16), g_over)
                dk = dot_nt(ds, q_over)
                dq_h += dot(k_hat_t[head_rows, part], ds)
                if h == 0:
                    dv_sum[part, lanes] = dv
                    dk_sum[part, lanes] = dk
                else:
                    dv_sum[part, lanes] += dv
                    dk_sum[part, lanes] += dk
            dq_t[head_rows, :] = dq_h * (over * (1.0 / math.sqrt(DH)))
        return carry

    lax.fori_loop(0, pairs, head_pair, 0)

    def norm_back(unit, inv, upstream):
        inner = dot((unit * upstream).astype(BF16), head_mean)
        return inv * (upstream - unit * inner)

    dq_low = norm_back(q_unit[...], q_inv[...], dq_t[...].T * gain_ref[0:1, :]).astype(BF16)
    for b in range(blocks):
        part = pl.ds(b * rows, rows)
        upstream = dk_sum[part, :] * gain_ref[1:2, :]
        dk_low[part, :] = norm_back(k_unit[part, :], k_inv[part, :], upstream).astype(BF16)
        dv_low[part, :] = dv_sum[part, :].astype(BF16)

    half = width // 2
    for target, near in ((send_ref, 1 - core), (keep_ref, core)):
        wanted = pl.ds(pl.multiple_of(near * half, half), half)
        w_q, w_k, w_v = (weight_ref[c, wanted, :] for c in range(3))
        for b in range(blocks):
            part = pl.ds(b * rows, rows)
            term = dot_nt(dk_low[part, :], w_k) + dot_nt(dv_low[part, :], w_v)
            if b == 0:
                term += dot_nt(dq_low, w_q)
                first = N * SLAB
                target[first : first + rows, :] = term[:, : half // 2].astype(BF16)
                target[first + rows : first + 2 * rows, :] = term[:, half // 2 :].astype(BF16)
            else:
                target[(b - 1) * BLOCK : b * BLOCK, :] = slabbed(term, half // 2).astype(BF16)

    piece = cols // 4
    per_x = width // AX
    for c in range(3):
        for i in range(AX):
            mine = slice(i * per_x, (i + 1) * per_x)
            if c == 0:
                term = dot(feats_t[mine, 0:rows], dq_low)
            elif c == 1:
                term = dot(feats_t[mine, :], dk_low[...])
            else:
                term = dot(feats_t[mine, :], dv_low[...])
            term = term.reshape(AZ, AY, CAP, cols)
            for j in range(AY):
                strip = term[:, j].reshape(AZ * CAP, cols)
                first_ref[i, c, j] = slabbed(strip[:, : 2 * piece], piece).astype(BF16)
                second_ref[j, c, i] = slabbed(strip[:, 2 * piece :], piece).astype(BF16)


def layer(lists, valid, feats, table, weight, gain, grad):
    rows, width = feats.shape
    cols = grad.shape[1]
    keys = rows + table.shape[0]
    vmem = pl.BlockSpec(memory_space=pltpu.VMEM)
    smem = pl.BlockSpec(memory_space=pltpu.SMEM)
    strip = AZ * SLAB
    terms = N * SLAB + 2 * rows
    return pl.pallas_call(
        layer_kernel,
        out_shape=[
            jax.ShapeDtypeStruct((AX, 3, AY, strip, cols // 4), BF16),
            jax.ShapeDtypeStruct((AY, 3, AX, strip, cols // 4), BF16),
            jax.ShapeDtypeStruct((terms, width // 4), BF16),
            jax.ShapeDtypeStruct((terms, width // 4), BF16),
        ],
        in_specs=[smem, smem] + [vmem] * 5,
        out_specs=[vmem] * 4,
        scratch_shapes=[
            pltpu.VMEM((width, keys), BF16),
            pltpu.VMEM((keys, cols), BF16),
            pltpu.VMEM((cols, keys), BF16),
            pltpu.VMEM((keys, cols), F32),
            pltpu.VMEM((keys, cols), F32),
            pltpu.VMEM((keys, cols), BF16),
            pltpu.VMEM((rows, cols), F32),
            pltpu.VMEM((rows, cols), F32),
            pltpu.VMEM((cols, rows), F32),
            pltpu.VMEM((cols, rows), F32),
            pltpu.VMEM((keys, rows), F32),
            pltpu.VMEM((2, keys, rows), F32),
            pltpu.VMEM((2, keys, rows), F32),
            pltpu.VMEM((cols, rows), F32),
            pltpu.VMEM((keys, cols), F32),
            pltpu.VMEM((keys, cols), F32),
            pltpu.VMEM((keys, cols), BF16),
            pltpu.VMEM((keys, cols), BF16),
        ],
        compiler_params=pltpu.CompilerParams(vmem_limit_bytes=60 * 1024 * 1024),
        name="layer",
    )(lists, valid, feats, table, weight, gain, grad)


def axis_copies(src_of, landing, send_sems, recv_sems, axis_size, peer_of):
    copies = []
    for step in range(1, axis_size):
        copy = pltpu.make_async_remote_copy(
            src_ref=src_of(step),
            dst_ref=landing.at[step - 1],
            send_sem=send_sems.at[step - 1],
            recv_sem=recv_sems.at[step - 1],
            device_id={"dom": peer_of(step)},
            device_id_type=MESH,
        )
        copy.start()
        copies.append(copy)
    return copies


def reduce_kernel(
    idx_ref,
    first_ref,
    second_ref,
    keep_ref,
    send_ref,
    proj_ref,
    input_ref,
    pair_land,
    outgoing,
    landed,
    a_land,
    b_land,
    a_held,
    b_held,
    a_land2,
    b_land2,
    a_held2,
    b_held2,
    a_land3,
    b_land3,
    send_sem,
    recv_sem,
    pair_send,
    pair_recv,
    a_send,
    a_recv,
    b_send,
    b_recv,
    a_send2,
    a_recv2,
    b_send2,
    b_recv2,
    a_send3,
    a_recv3,
    b_send3,
    b_recv3,
):
    mine = place()
    dom, core, x, z, y = mine
    barrier = greet_all(dom, core)
    quarter = keep_ref.shape[1]
    own_rows = keep_ref.shape[0] - N * SLAB

    def at_x(step):
        return lax.rem(x + step, AX)

    def at_y(step):
        return lax.rem(y + step, AY)

    def at_z(step):
        return lax.rem(z + step, AZ)

    def peer_x(step):
        return at_x(step) * (AZ * AY) + z * AY + y

    def peer_y(step):
        return x * (AZ * AY) + z * AY + at_y(step)

    def peer_z(step):
        return x * (AZ * AY) + at_z(step) * AY + y

    pl.semaphore_wait(barrier, N)
    pairs = []
    for step in range(AX + 1):
        if step < AX:
            part = rows_at(at_x(step) * BLOCK, BLOCK)
        else:
            part = pl.ds(N * SLAB, own_rows)
        pair = pltpu.make_async_remote_copy(
            src_ref=send_ref.at[part],
            dst_ref=pair_land.at[part],
            send_sem=pair_send.at[step],
            recv_sem=pair_recv.at[step],
            device_id={"mp": 1 - core},
            device_id_type=MESH,
        )
        pair.start()
        pairs.append(pair)
    a_copies = axis_copies(lambda s: first_ref.at[at_x(s)], a_land, a_send, a_recv, AX, peer_x)
    b_copies = axis_copies(lambda s: second_ref.at[at_y(s)], b_land, b_send, b_recv, AY, peer_y)
    for step in range(AX):
        part = rows_at(at_x(step) * BLOCK, BLOCK)
        pairs[step].wait()
        outgoing[part, :] = (keep_ref[part, :].astype(F32) + pair_land[part, :].astype(F32)).astype(BF16)
        push_block(step, mine, outgoing, landed, send_sem, recv_sem)
    own = rows_at(dom * SLAB, SLAB)
    landed[own, :] = outgoing[own, :]

    def total(own_part, landing):
        result = own_part.astype(F32)
        for s in range(landing.shape[0]):
            result += landing[s].astype(F32)
        return result

    for copy in a_copies:
        copy.wait()
    a_held[...] = total(first_ref[x], a_land).astype(BF16)
    a_copies = axis_copies(lambda s: a_held.at[:, at_y(s)], a_land2, a_send2, a_recv2, AY, peer_y)
    for copy in b_copies:
        copy.wait()
    b_held[...] = total(second_ref[y], b_land).astype(BF16)
    b_copies = axis_copies(lambda s: b_held.at[:, at_x(s)], b_land2, b_send2, b_recv2, AX, peer_x)
    for copy in a_copies:
        copy.wait()
    a_held2[...] = total(a_held[:, y], a_land2).astype(BF16)
    a_copies = axis_copies(
        lambda s: a_held2.at[:, rows_at(at_z(s) * SLAB, SLAB)], a_land3, a_send3, a_recv3, AZ, peer_z
    )
    for copy in b_copies:
        copy.wait()
    b_held2[...] = total(b_held[:, x], b_land2).astype(BF16)
    b_copies = axis_copies(
        lambda s: b_held2.at[:, rows_at(at_z(s) * SLAB, SLAB)], b_land3, b_send3, b_recv3, AZ, peer_z
    )

    pairs[AX].wait()
    fixed = pl.ds(N * SLAB, own_rows)
    result = keep_ref[fixed, :].astype(F32) + pair_land[fixed, :].astype(F32)
    for step in range(AX):
        near = lax.rem(x - step + AX, AX)
        if step == 0:
            wait_bytes(landed.at[pl.ds(0, BLOCK - SLAB)], recv_sem.at[step])
        else:
            wait_bytes(landed.at[rows_at(near * BLOCK, BLOCK)], recv_sem.at[step])
        kinds = lax.broadcasted_iota(jnp.int32, (own_rows, BLOCK), 0)
        pick = jnp.where(kinds == idx_ref[near], 1.0, 0.0).astype(BF16)
        result += dot(pick, landed[rows_at(near * BLOCK, BLOCK), :])
    input_ref[:, 0:quarter] = result[: own_rows // 2].astype(BF16)
    input_ref[:, quarter:] = result[own_rows // 2 :].astype(BF16)

    piece = a_land3.shape[3]
    mine_z = rows_at(z * SLAB, SLAB)
    for copy in a_copies:
        copy.wait()
    done = total(a_held2[:, mine_z, :], a_land3)
    proj_ref[:, :, 0:piece] = done[:, :CAP]
    proj_ref[:, :, piece : 2 * piece] = done[:, CAP:]
    for copy in b_copies:
        copy.wait()
    done = total(b_held2[:, mine_z, :], b_land3)
    proj_ref[:, :, 2 * piece : 3 * piece] = done[:, :CAP]
    proj_ref[:, :, 3 * piece :] = done[:, CAP:]
    wait_bytes(outgoing.at[pl.ds(0, (N - 1) * SLAB)], send_sem)


def reduce_all(idx, first, second, keep, send):
    terms, quarter = keep.shape
    strip, piece = first.shape[3:]
    vmem = pl.BlockSpec(memory_space=pltpu.VMEM)
    dma = pltpu.SemaphoreType.DMA
    return pl.pallas_call(
        reduce_kernel,
        out_shape=[
            jax.ShapeDtypeStruct((3, CAP, 4 * piece), F32),
            jax.ShapeDtypeStruct(((terms - N * SLAB) // 2, 2 * quarter), BF16),
        ],
        in_specs=[vmem] * 5,
        out_specs=[vmem] * 2,
        scratch_shapes=[
            pltpu.VMEM((terms, quarter), BF16),
            pltpu.VMEM((N * SLAB, quarter), BF16),
            pltpu.VMEM((N * SLAB, quarter), BF16),
            pltpu.VMEM((AX - 1, 3, AY, strip, piece), BF16),
            pltpu.VMEM((AY - 1, 3, AX, strip, piece), BF16),
            pltpu.VMEM((3, AY, strip, piece), BF16),
            pltpu.VMEM((3, AX, strip, piece), BF16),
            pltpu.VMEM((AY - 1, 3, strip, piece), BF16),
            pltpu.VMEM((AX - 1, 3, strip, piece), BF16),
            pltpu.VMEM((3, strip, piece), BF16),
            pltpu.VMEM((3, strip, piece), BF16),
            pltpu.VMEM((AZ - 1, 3, SLAB, piece), BF16),
            pltpu.VMEM((AZ - 1, 3, SLAB, piece), BF16),
            dma,
            dma((AX,)),
            dma((AX + 1,)),
            dma((AX + 1,)),
            dma((AX - 1,)),
            dma((AX - 1,)),
            dma((AY - 1,)),
            dma((AY - 1,)),
            dma((AY - 1,)),
            dma((AY - 1,)),
            dma((AX - 1,)),
            dma((AX - 1,)),
            dma((AZ - 1,)),
            dma((AZ - 1,)),
            dma((AZ - 1,)),
            dma((AZ - 1,)),
        ],
        compiler_params=pltpu.CompilerParams(
            collective_id=1, has_side_effects=True, vmem_limit_bytes=40 * 1024 * 1024
        ),
        name="reduce_all",
    )(idx, first, second, keep, send)


def body(
    node_feats, proj_weight, norm_gain, grad_out, tile_lists, tile_valid, send_rows, send_count
):
    rows = node_feats.shape[0]
    live = jnp.arange(CAP, dtype=jnp.int32)[None, :] < send_count.reshape(N, 1)
    left = jnp.where(live, send_rows, 2 * rows)
    right = jnp.where(live, send_rows + rows, 2 * rows)
    idx = jnp.concatenate([left, right], axis=1).reshape(AX, 1, BLOCK)
    weight = jnp.transpose(proj_weight, (1, 0, 2))
    table = fetch(idx, node_feats)
    first, second, keep, send = layer(
        tile_lists, tile_valid, node_feats, table, weight, norm_gain, grad_out
    )
    proj_grad, input_grad = reduce_all(idx, first, second, keep, send)
    return (jnp.transpose(proj_grad, (1, 0, 2)), input_grad)


def solution(mesh):
    in_specs = (
        P("dom", None),
        P(None, None, "mp"),
        P(None, "mp"),
        P("dom", "mp"),
        P("dom", None),
        P("dom"),
        P("dom", None),
        P("dom", None),
    )
    out_specs = (P("dom", None, "mp"), P("dom", "mp"))
    return jax.shard_map(body, mesh=mesh, in_specs=in_specs, out_specs=out_specs, check_vma=False)
```

```python
import math

import jax
import jax.numpy as jnp
from jax import lax
from jax.experimental import pallas as pl
from jax.experimental.pallas import tpu as pltpu
from jax.sharding import PartitionSpec as P

DH = 64
TILE = 128
CAP = 8
SLAB = 2 * CAP
EPS = 1e-06
AX, AZ, AY = 4, 8, 4
N = AX * AZ * AY
DEAD = 1024.0
LIVE_MAX = 512.0
LOG2E = math.log2(math.e)
MESH = pl.DeviceIdType.MESH
F32 = jnp.float32
BF16 = jnp.bfloat16


def dot(a, b):
    return jnp.dot(a, b, preferred_element_type=F32)


def dot_nt(a, b):
    return lax.dot_general(a, b, (((1,), (1,)), ((), ())), preferred_element_type=F32)


def dot_tn(a, b):
    return lax.dot_general(a, b, (((0,), (0,)), ((), ())), preferred_element_type=F32)


def place():
    dom = lax.axis_index("dom")
    core = lax.axis_index("mp")
    return dom, core, dom // (AZ * AY), lax.rem(dom // AY, AZ), lax.rem(dom, AY)


def rows_at(start, size):
    return pl.ds(pl.multiple_of(start, SLAB), size)


def greet_all(dom, core):
    barrier = pltpu.get_barrier_semaphore()

    def greet(i, carry):
        peer = lax.rem(dom + 1 + i, N)
        pl.semaphore_signal(barrier, inc=1, device_id={"dom": peer}, device_id_type=MESH)
        return carry

    lax.fori_loop(0, N - 1, greet, 0)
    pl.semaphore_signal(barrier, inc=1, device_id={"mp": 1 - core}, device_id_type=MESH)
    return barrier


def wait_bytes(ref, sem):
    pltpu.make_async_copy(ref, ref, sem).wait()


BLOCK = AZ * AY * SLAB
BLOCK_KEYS = AZ * AY * CAP


def push_block(step, mine, src, dst, send_sem, recv_sem):
    dom, core, x, z, y = mine
    far = lax.rem(x + step, AX)

    def push(i, carry):
        dz, dy = i // AY, lax.rem(i, AY)
        peer = far * (AZ * AY) + lax.rem(z + dz, AZ) * AY + lax.rem(y + dy, AY)
        pltpu.make_async_remote_copy(
            src_ref=src.at[rows_at(peer * SLAB, SLAB)],
            dst_ref=dst.at[rows_at(dom * SLAB, SLAB)],
            send_sem=send_sem,
            recv_sem=recv_sem.at[step],
            device_id={"dom": peer},
            device_id_type=MESH,
        ).start()
        return carry

    lax.fori_loop(1 if step == 0 else 0, AZ * AY, push, 0)


def wait_block(step, near, landed, recv_sem):
    if step == 0:
        wait_bytes(landed.at[pl.ds(0, BLOCK - SLAB)], recv_sem.at[step])
    else:
        wait_bytes(landed.at[rows_at(near * BLOCK, BLOCK)], recv_sem.at[step])


def to_other_core(src, dst, core, send_sem, recv_sem):
    copy = pltpu.make_async_remote_copy(
        src_ref=src,
        dst_ref=dst,
        send_sem=send_sem,
        recv_sem=recv_sem,
        device_id={"mp": 1 - core},
        device_id_type=MESH,
    )
    copy.start()
    return copy


def slabbed(block, width):
    count = block.shape[0] // CAP
    left = block[:, :width].reshape(count, CAP, width)
    right = block[:, width:].reshape(count, CAP, width)
    return jnp.concatenate([left, right], axis=1).reshape(count * SLAB, width)


def axis_copy(step, src, landing, send_sems, recv_sems, peer):
    copy = pltpu.make_async_remote_copy(
        src_ref=src,
        dst_ref=landing.at[step - 1],
        send_sem=send_sems.at[step - 1],
        recv_sem=recv_sems.at[step - 1],
        device_id={"dom": peer},
        device_id_type=MESH,
    )
    copy.start()
    return copy


def total_of(own_part, landing):
    result = own_part.astype(F32)
    for s in range(landing.shape[0]):
        result += landing[s].astype(F32)
    return result


def layer_kernel(
    lists_ref,
    valid_ref,
    idx_ref,
    feats_ref,
    weight_ref,
    gain_ref,
    grad_ref,
    proj_ref,
    input_ref,
    halves,
    outgoing,
    landed,
    feats_t,
    k_hat,
    k_hat_t,
    k_unit,
    k_inv,
    values,
    q_unit,
    q_inv,
    q_t,
    g_t,
    q_head,
    g_head,
    mask_t,
    expo,
    expo_dp,
    total,
    moment,
    dq_t,
    dk_sum,
    dk_low,
    dv_low,
    dq_low,
    keep,
    give,
    pair_land,
    back,
    back_land,
    first,
    second,
    a_land,
    b_land,
    a_held,
    b_held,
    a_land2,
    b_land2,
    a_held2,
    b_held2,
    a_land3,
    b_land3,
    send_sem,
    recv_sem,
    half_send,
    half_recv,
    pair_send,
    pair_recv,
    back_send,
    back_recv,
    a_send,
    a_recv,
    b_send,
    b_recv,
    a_send2,
    a_recv2,
    b_send2,
    b_recv2,
    a_send3,
    a_recv3,
    b_send3,
    b_recv3,
):
    mine = place()
    dom, core, x, z, y = mine
    barrier = greet_all(dom, core)
    rows, width = feats_ref.shape
    cols = grad_ref.shape[1]
    half = width // 2
    quarter = half // 2
    heads = cols // DH
    own_slab = rows_at(dom * SLAB, SLAB)
    own_tiles = rows // TILE

    def at_x(step):
        return lax.rem(x + step, AX)

    def at_y(step):
        return lax.rem(y + step, AY)

    def at_z(step):
        return lax.rem(z + step, AZ)

    def peer_x(step):
        return at_x(step) * (AZ * AY) + z * AY + y

    def peer_y(step):
        return x * (AZ * AY) + z * AY + at_y(step)

    def peer_z(step):
        return x * (AZ * AY) + at_z(step) * AY + y

    halves[0:rows, :] = feats_ref[:, pl.ds(pl.multiple_of(core * half, half), quarter)]
    halves[rows : 2 * rows, :] = feats_ref[
        :, pl.ds(pl.multiple_of(core * half + quarter, quarter), quarter)
    ]
    halves[2 * rows :, :] = jnp.full((SLAB, quarter), DEAD, BF16)
    for step in range(AX):
        far = at_x(step)
        kinds = lax.broadcasted_iota(jnp.int32, (2 * rows + SLAB, BLOCK), 0)
        pick = jnp.where(kinds == idx_ref[far], 1.0, 0.0).astype(BF16)
        outgoing[rows_at(far * BLOCK, BLOCK), :] = dot_tn(pick, halves[...]).astype(BF16)
        if step == 0:
            pl.semaphore_wait(barrier, N)
        push_block(step, mine, outgoing, landed.at[core], send_sem, recv_sem)
    landed[core, own_slab, :] = outgoing[own_slab, :]

    head_of = lax.broadcasted_iota(jnp.int32, (cols, cols), 0) // DH
    head_to = lax.broadcasted_iota(jnp.int32, (cols, cols), 1) // DH
    head_mean = jnp.where(head_of == head_to, 1.0 / DH, 0.0).astype(BF16)
    which = lax.broadcasted_iota(jnp.int32, (2 * DH, rows), 0) // DH

    def part_of(b):
        return pl.ds(b * rows, rows)

    def lanes_of(pair):
        return pl.ds(pl.multiple_of(pair * 2 * DH, 2 * DH), 2 * DH)

    def normed(mixed):
        inv = lax.rsqrt(dot((mixed * mixed).astype(BF16), head_mean) + EPS)
        return mixed * inv, inv

    def consume(b, block, tile_live, first_tile):
        part = part_of(b)
        feats_t[:, part] = block.T
        unit, inv = normed(dot(block, weight_ref[1]))
        k_inv[part, :] = inv
        k_unit[part, :] = unit
        low = (unit * gain_ref[1:2, :]).astype(BF16)
        k_hat[part, :] = low
        k_hat_t[:, part] = low.T
        values[part, :] = dot(block, weight_ref[2]).astype(BF16)
        for j in range(own_tiles):
            for t in range(own_tiles):
                listed = jnp.int32(0)
                for i in range(lists_ref.shape[1]):
                    listed += jnp.where(lists_ref[t, i] == first_tile + j, 1, 0)
                mask_t[j * TILE : (j + 1) * TILE, t * TILE : (t + 1) * TILE] = (
                    tile_live(j) * listed.astype(F32)
                )

        def head_pair(pair, carry):
            lanes = lanes_of(pair)
            k_pair = k_hat[part, lanes]
            v_pair = values[part, lanes]
            for h in range(2):
                head = pair * 2 + h
                low = (jnp.exp2(dot(k_pair, q_head[head])) * mask_t[...]).astype(BF16)
                expo[head, part, :] = low
                e = low.astype(F32)
                e_dp = e * dot(v_pair, g_head[head])
                expo_dp[head, part, :] = e_dp
                if b == 0:
                    total[head] = jnp.sum(e, axis=0, keepdims=True)
                    moment[head] = jnp.sum(e_dp, axis=0, keepdims=True)
                else:
                    total[head] += jnp.sum(e, axis=0, keepdims=True)
                    moment[head] += jnp.sum(e_dp, axis=0, keepdims=True)
            return carry

        lax.fori_loop(0, heads // 2, head_pair, 0)

    own_block = feats_ref[...]
    unit, inv = normed(dot(own_block, weight_ref[0]))
    q_inv[...] = inv
    q_unit[...] = unit
    q_t[...] = (unit * (gain_ref[0:1, :] * (LOG2E / math.sqrt(DH)))).T
    g_t[...] = grad_ref[...].astype(F32).T
    for head in range(heads):
        lanes = pl.ds(head // 2 * 2 * DH, 2 * DH)
        q_head[head] = jnp.where(which == head % 2, q_t[lanes, :], 0.0).astype(BF16)
        g_head[head] = jnp.where(which == head % 2, g_t[lanes, :], 0.0).astype(BF16)
    place_in_tile = lax.broadcasted_iota(jnp.int32, (TILE, TILE), 0)
    consume(0, own_block, lambda j: jnp.where(place_in_tile < valid_ref[j], 1.0, 0.0), 0)

    for step in range(AX):
        near = lax.rem(x - step + AX, AX)
        wait_block(step, near, landed.at[core], recv_sem)
        arrived = landed.at[core, rows_at(near * BLOCK, BLOCK)]
        pair = to_other_core(arrived, arrived, core, half_send.at[step], half_recv.at[step])
        pair.wait()
        strips = []
        for plane in range(2):
            slabs = landed[plane, rows_at(near * BLOCK, BLOCK), :].astype(F32)
            slabs = slabs.reshape(AZ * AY, SLAB, quarter)
            strips.append(slabs[:, :CAP, :].reshape(BLOCK_KEYS, quarter))
            strips.append(slabs[:, CAP:, :].reshape(BLOCK_KEYS, quarter))
        mark = strips[0][:, 0:1]

        def received_live(j):
            column = jnp.broadcast_to(mark[j * TILE : (j + 1) * TILE], (TILE, TILE))
            return jnp.where(column < LIVE_MAX, 1.0, 0.0)

        block = jnp.concatenate([strip.astype(BF16) for strip in strips], axis=1)
        consume(step + 1, block, received_live, own_tiles + near * own_tiles)

    for head in range(heads):
        lanes = pl.ds(head // 2 * 2 * DH, 2 * DH)
        over = 1.0 / total[head]
        moment[head] = moment[head] * over
        total[head] = over
        q_head[head] = jnp.where(
            which == head % 2, q_t[lanes, :] * (over * (1.0 / LOG2E)), 0.0
        ).astype(BF16)
        g_head[head] = jnp.where(which == head % 2, g_t[lanes, :] * over, 0.0).astype(BF16)

    def norm_back(unit, inv, upstream):
        inner = dot((unit * upstream).astype(BF16), head_mean)
        return inv * (upstream - unit * inner)

    pairs = []
    fixed = pl.ds(N * SLAB, 2 * rows)

    def finish(step):
        near = lax.rem(x - step + AX, AX)
        part = rows_at(near * BLOCK, BLOCK)
        local = pl.ds(step * BLOCK, BLOCK)
        pairs[step].wait()
        back[part, :] = (keep[local, :] + pair_land[local, :].astype(F32)).astype(BF16)
        push_block((AX - step) % AX, mine, back, back_land, back_send, back_recv)

    for step in range(AX + 1):
        b = (step + 1) % (AX + 1)
        part = part_of(b)

        def head_pair(pair, carry):
            lanes = lanes_of(pair)
            lows, slopes = [], []
            for h in range(2):
                head = pair * 2 + h
                low = expo[head, part, :]
                ds = (expo_dp[head, part, :] - low.astype(F32) * moment[head]).astype(BF16)
                head_rows = pl.ds(pl.multiple_of(head * DH, DH), DH)
                dq = dot(k_hat_t[head_rows, part], ds)
                if step == 0:
                    dq_t[head_rows, :] = dq
                else:
                    dq_t[head_rows, :] += dq
                lows.append(low)
                slopes.append(ds)
            g_both = jnp.concatenate([g_head[pair * 2], g_head[pair * 2 + 1]], axis=1)
            q_both = jnp.concatenate([q_head[pair * 2], q_head[pair * 2 + 1]], axis=1)
            dv_low[part, lanes] = dot_nt(jnp.concatenate(lows, axis=1), g_both).astype(BF16)
            dk_sum[:, lanes] = dot_nt(jnp.concatenate(slopes, axis=1), q_both)
            return carry

        lax.fori_loop(0, heads // 2, head_pair, 0)
        upstream = dk_sum[...] * gain_ref[1:2, :]
        dk_low[part, :] = norm_back(k_unit[part, :], k_inv[part, :], upstream).astype(BF16)
        if b == 0:
            for head in range(heads):
                head_rows = slice(head * DH, (head + 1) * DH)
                dq_t[head_rows, :] = dq_t[head_rows, :] * (total[head] * (1.0 / math.sqrt(DH)))
            upstream = dq_t[...].T * gain_ref[0:1, :]
            dq_low[...] = norm_back(q_unit[...], q_inv[...], upstream).astype(BF16)
        local = pl.ds(step * BLOCK, BLOCK)
        for side in range(2):
            near = core if side else 1 - core
            wanted = pl.ds(pl.multiple_of(near * half, half), half)
            term = dot_nt(dk_low[part, :], weight_ref[1, wanted, :])
            term += dot_nt(dv_low[part, :], weight_ref[2, wanted, :])
            if b == 0:
                term += dot_nt(dq_low[...], weight_ref[0, wanted, :])
                term = jnp.concatenate([term[:, :quarter], term[:, quarter:]], axis=0)
            else:
                term = slabbed(term, quarter)
            if side:
                keep[local, :] = term
            else:
                give[local, :] = term.astype(BF16)
                pairs.append(
                    to_other_core(
                        give.at[local],
                        pair_land.at[local],
                        core,
                        pair_send.at[step],
                        pair_recv.at[step],
                    )
                )
        if step > 0:
            finish(step - 1)
    back_land[own_slab, :] = back[own_slab, :]

    piece = cols // 4
    per_x = width // AX
    a_copies = []
    for step in (1, 2, 3, 0):
        i = at_x(step)
        chunk = pl.ds(pl.multiple_of(i * per_x, per_x), per_x)
        for c in range(3):
            if c == 0:
                term = dot(feats_t[chunk, 0:rows], dq_low[...])
            elif c == 1:
                term = dot(feats_t[chunk, :], dk_low[...])
            else:
                term = dot(feats_t[chunk, :], dv_low[...])
            term = term.reshape(AZ, AY, CAP, cols)
            for j in range(AY):
                strip = term[:, j].reshape(AZ * CAP, cols)
                first[i, c, j] = slabbed(strip[:, : 2 * piece], piece).astype(BF16)
                second[j, c, i] = slabbed(strip[:, 2 * piece :], piece).astype(BF16)
        if step > 0:
            a_copies.append(axis_copy(step, first.at[i], a_land, a_send, a_recv, peer_x(step)))
    b_copies = [
        axis_copy(s, second.at[at_y(s)], b_land, b_send, b_recv, peer_y(s)) for s in range(1, AY)
    ]

    for copy in a_copies:
        copy.wait()
    a_held[...] = total_of(first[x], a_land).astype(BF16)
    a_copies = [
        axis_copy(s, a_held.at[:, at_y(s)], a_land2, a_send2, a_recv2, peer_y(s))
        for s in range(1, AY)
    ]
    for copy in b_copies:
        copy.wait()
    b_held[...] = total_of(second[y], b_land).astype(BF16)
    b_copies = [
        axis_copy(s, b_held.at[:, at_x(s)], b_land2, b_send2, b_recv2, peer_x(s))
        for s in range(1, AX)
    ]
    for copy in a_copies:
        copy.wait()
    a_held2[...] = total_of(a_held[:, y], a_land2).astype(BF16)
    a_copies = [
        axis_copy(s, a_held2.at[:, rows_at(at_z(s) * SLAB, SLAB)], a_land3, a_send3, a_recv3, peer_z(s))
        for s in range(1, AZ)
    ]
    for copy in b_copies:
        copy.wait()
    b_held2[...] = total_of(b_held[:, x], b_land2).astype(BF16)
    b_copies = [
        axis_copy(s, b_held2.at[:, rows_at(at_z(s) * SLAB, SLAB)], b_land3, b_send3, b_recv3, peer_z(s))
        for s in range(1, AZ)
    ]

    pairs[AX].wait()
    local = pl.ds(AX * BLOCK, 2 * rows)
    result = keep[local, :] + pair_land[local, :].astype(F32)
    for step in (0, 3, 2, 1):
        near = lax.rem(x - step + AX, AX)
        wait_block(step, near, back_land, back_recv)
        kinds = lax.broadcasted_iota(jnp.int32, (2 * rows, BLOCK), 0)
        pick = jnp.where(kinds == idx_ref[near], 1.0, 0.0).astype(BF16)
        result += dot(pick, back_land[rows_at(near * BLOCK, BLOCK), :])
    input_ref[:, 0:quarter] = result[:rows].astype(BF16)
    input_ref[:, quarter:] = result[rows:].astype(BF16)

    mine_z = rows_at(z * SLAB, SLAB)
    for copy in a_copies:
        copy.wait()
    done = total_of(a_held2[:, mine_z, :], a_land3)
    proj_ref[:, :, 0:piece] = done[:, :CAP]
    proj_ref[:, :, piece : 2 * piece] = done[:, CAP:]
    for copy in b_copies:
        copy.wait()
    done = total_of(b_held2[:, mine_z, :], b_land3)
    proj_ref[:, :, 2 * piece : 3 * piece] = done[:, :CAP]
    proj_ref[:, :, 3 * piece :] = done[:, CAP:]
    wait_bytes(outgoing.at[pl.ds(0, (N - 1) * SLAB)], send_sem)
    wait_bytes(back.at[pl.ds(0, (N - 1) * SLAB)], back_send)


def layer(lists, valid, idx, feats, weight, gain, grad):
    rows, width = feats.shape
    cols = grad.shape[1]
    heads = cols // DH
    keys = rows + N * CAP
    quarter = width // 4
    piece = cols // 4
    strip = AZ * SLAB
    terms = N * SLAB + 2 * rows
    smem = pl.BlockSpec(memory_space=pltpu.SMEM)
    vmem = pl.BlockSpec(memory_space=pltpu.VMEM)
    ram = pltpu.VMEM
    dma = pltpu.SemaphoreType.DMA
    return pl.pallas_call(
        layer_kernel,
        out_shape=[
            jax.ShapeDtypeStruct((3, CAP, cols), F32),
            jax.ShapeDtypeStruct((rows, half_of(width)), BF16),
        ],
        in_specs=[smem, smem] + [vmem] * 5,
        out_specs=[vmem] * 2,
        scratch_shapes=[
            ram((2 * rows + SLAB, quarter), BF16),
            ram((N * SLAB, quarter), BF16),
            ram((2, N * SLAB, quarter), BF16),
            ram((width, keys), BF16),
            ram((keys, cols), BF16),
            ram((cols, keys), BF16),
            ram((keys, cols), F32),
            ram((keys, cols), F32),
            ram((keys, cols), BF16),
            ram((rows, cols), F32),
            ram((rows, cols), F32),
            ram((cols, rows), F32),
            ram((cols, rows), F32),
            ram((heads, 2 * DH, rows), BF16),
            ram((heads, 2 * DH, rows), BF16),
            ram((rows, rows), F32),
            ram((heads, keys, rows), BF16),
            ram((heads, keys, rows), F32),
            ram((heads, 1, rows), F32),
            ram((heads, 1, rows), F32),
            ram((cols, rows), F32),
            ram((rows, cols), F32),
            ram((keys, cols), BF16),
            ram((keys, cols), BF16),
            ram((rows, cols), BF16),
            ram((terms, quarter), F32),
            ram((terms, quarter), BF16),
            ram((terms, quarter), BF16),
            ram((N * SLAB, quarter), BF16),
            ram((N * SLAB, quarter), BF16),
            ram((AX, 3, AY, strip, piece), BF16),
            ram((AY, 3, AX, strip, piece), BF16),
            ram((AX - 1, 3, AY, strip, piece), BF16),
            ram((AY - 1, 3, AX, strip, piece), BF16),
            ram((3, AY, strip, piece), BF16),
            ram((3, AX, strip, piece), BF16),
            ram((AY - 1, 3, strip, piece), BF16),
            ram((AX - 1, 3, strip, piece), BF16),
            ram((3, strip, piece), BF16),
            ram((3, strip, piece), BF16),
            ram((AZ - 1, 3, SLAB, piece), BF16),
            ram((AZ - 1, 3, SLAB, piece), BF16),
            dma,
            dma((AX,)),
            dma((AX,)),
            dma((AX,)),
            dma((AX + 1,)),
            dma((AX + 1,)),
            dma,
            dma((AX,)),
            dma((AX - 1,)),
            dma((AX - 1,)),
            dma((AY - 1,)),
            dma((AY - 1,)),
            dma((AY - 1,)),
            dma((AY - 1,)),
            dma((AX - 1,)),
            dma((AX - 1,)),
            dma((AZ - 1,)),
            dma((AZ - 1,)),
            dma((AZ - 1,)),
            dma((AZ - 1,)),
        ],
        compiler_params=pltpu.CompilerParams(
            collective_id=0, has_side_effects=True, vmem_limit_bytes=60 * 1024 * 1024
        ),
        name="layer",
    )(lists, valid, idx, feats, weight, gain, grad)


def half_of(size):
    return size // 2


def body(
    node_feats, proj_weight, norm_gain, grad_out, tile_lists, tile_valid, send_rows, send_count
):
    rows = node_feats.shape[0]
    live = jnp.arange(CAP, dtype=jnp.int32)[None, :] < send_count.reshape(N, 1)
    left = jnp.where(live, send_rows, 2 * rows)
    right = jnp.where(live, send_rows + rows, 2 * rows)
    idx = jnp.concatenate([left, right], axis=1).reshape(AX, 1, BLOCK)
    weight = jnp.transpose(proj_weight, (1, 0, 2))
    proj_grad, input_grad = layer(
        tile_lists, tile_valid, idx, node_feats, weight, norm_gain, grad_out
    )
    return (jnp.transpose(proj_grad, (1, 0, 2)), input_grad)


def solution(mesh):
    in_specs = (
        P("dom", None),
        P(None, None, "mp"),
        P(None, "mp"),
        P("dom", "mp"),
        P("dom", None),
        P("dom"),
        P("dom", None),
        P("dom", None),
    )
    out_specs = (P("dom", None, "mp"), P("dom", "mp"))
    return jax.shard_map(body, mesh=mesh, in_specs=in_specs, out_specs=out_specs, check_vma=False)
```

```python
import math

import jax
import jax.numpy as jnp
from jax import lax
from jax.experimental import pallas as pl
from jax.experimental.pallas import tpu as pltpu
from jax.sharding import PartitionSpec as P

DH = 64
TILE = 128
CAP = 8
SLAB = 2 * CAP
EPS = 1e-06
AX, AZ, AY = 4, 8, 4
N = AX * AZ * AY
DEAD = 1024.0
LIVE_MAX = 512.0
LOG2E = math.log2(math.e)
MESH = pl.DeviceIdType.MESH
F32 = jnp.float32
BF16 = jnp.bfloat16


def dot(a, b):
    return jnp.dot(a, b, preferred_element_type=F32)


def dot_nt(a, b):
    return lax.dot_general(a, b, (((1,), (1,)), ((), ())), preferred_element_type=F32)


def dot_tn(a, b):
    return lax.dot_general(a, b, (((0,), (0,)), ((), ())), preferred_element_type=F32)


def place():
    dom = lax.axis_index("dom")
    core = lax.axis_index("mp")
    return dom, core, dom // (AZ * AY), lax.rem(dom // AY, AZ), lax.rem(dom, AY)


def rows_at(start, size):
    return pl.ds(pl.multiple_of(start, SLAB), size)


def greet_all(dom, core):
    barrier = pltpu.get_barrier_semaphore()

    def greet(i, carry):
        peer = lax.rem(dom + 1 + i, N)
        pl.semaphore_signal(barrier, inc=1, device_id={"dom": peer}, device_id_type=MESH)
        return carry

    lax.fori_loop(0, N - 1, greet, 0)
    pl.semaphore_signal(barrier, inc=1, device_id={"mp": 1 - core}, device_id_type=MESH)
    return barrier


def wait_bytes(ref, sem):
    pltpu.make_async_copy(ref, ref, sem).wait()


BLOCK = AZ * AY * SLAB
BLOCK_KEYS = AZ * AY * CAP


def push_block(step, mine, src, dst, send_sem, recv_sem):
    dom, core, x, z, y = mine
    far = lax.rem(x + step, AX)

    def push(i, carry):
        dz, dy = i // AY, lax.rem(i, AY)
        peer = far * (AZ * AY) + lax.rem(z + dz, AZ) * AY + lax.rem(y + dy, AY)
        pltpu.make_async_remote_copy(
            src_ref=src.at[rows_at(peer * SLAB, SLAB)],
            dst_ref=dst.at[rows_at(dom * SLAB, SLAB)],
            send_sem=send_sem,
            recv_sem=recv_sem.at[step],
            device_id={"dom": peer},
            device_id_type=MESH,
        ).start()
        return carry

    lax.fori_loop(1 if step == 0 else 0, AZ * AY, push, 0)


def wait_block(step, near, landed, recv_sem):
    if step == 0:
        wait_bytes(landed.at[pl.ds(0, BLOCK - SLAB)], recv_sem.at[step])
    else:
        wait_bytes(landed.at[rows_at(near * BLOCK, BLOCK)], recv_sem.at[step])


def to_other_core(src, dst, core, send_sem, recv_sem):
    copy = pltpu.make_async_remote_copy(
        src_ref=src,
        dst_ref=dst,
        send_sem=send_sem,
        recv_sem=recv_sem,
        device_id={"mp": 1 - core},
        device_id_type=MESH,
    )
    copy.start()
    return copy


def slabbed(block, width):
    count = block.shape[0] // CAP
    left = block[:, :width].reshape(count, CAP, width)
    right = block[:, width:].reshape(count, CAP, width)
    return jnp.concatenate([left, right], axis=1).reshape(count * SLAB, width)


def axis_copy(step, src, landing, send_sems, recv_sems, peer):
    copy = pltpu.make_async_remote_copy(
        src_ref=src,
        dst_ref=landing.at[step - 1],
        send_sem=send_sems.at[step - 1],
        recv_sem=recv_sems.at[step - 1],
        device_id={"dom": peer},
        device_id_type=MESH,
    )
    copy.start()
    return copy


def total_of(own_part, landing):
    result = own_part.astype(F32)
    for s in range(landing.shape[0]):
        result += landing[s].astype(F32)
    return result


def layer_kernel(
    lists_ref,
    valid_ref,
    idx_ref,
    feats_ref,
    weight_ref,
    gain_ref,
    grad_ref,
    proj_ref,
    input_ref,
    halves,
    outgoing,
    landed,
    feats_t,
    k_hat,
    k_hat_t,
    k_unit,
    k_inv,
    values,
    q_unit,
    q_inv,
    q_t,
    g_t,
    q_head,
    g_head,
    mask_t,
    expo,
    expo_dp,
    total,
    moment,
    dq_t,
    kv_low,
    dq_low,
    keep,
    give,
    pair_land,
    back,
    back_land,
    first,
    second,
    a_land,
    b_land,
    a_held,
    b_held,
    a_land2,
    b_land2,
    a_held2,
    b_held2,
    a_land3,
    b_land3,
    send_sem,
    recv_sem,
    half_send,
    half_recv,
    pair_send,
    pair_recv,
    back_send,
    back_recv,
    a_send,
    a_recv,
    b_send,
    b_recv,
    a_send2,
    a_recv2,
    b_send2,
    b_recv2,
    a_send3,
    a_recv3,
    b_send3,
    b_recv3,
):
    mine = place()
    dom, core, x, z, y = mine
    barrier = greet_all(dom, core)
    rows, width = feats_ref.shape
    cols = grad_ref.shape[1]
    half = width // 2
    quarter = half // 2
    heads = cols // DH
    own_slab = rows_at(dom * SLAB, SLAB)
    own_tiles = rows // TILE

    def at_x(step):
        return lax.rem(x + step, AX)

    def at_y(step):
        return lax.rem(y + step, AY)

    def at_z(step):
        return lax.rem(z + step, AZ)

    def peer_x(step):
        return at_x(step) * (AZ * AY) + z * AY + y

    def peer_y(step):
        return x * (AZ * AY) + z * AY + at_y(step)

    def peer_z(step):
        return x * (AZ * AY) + at_z(step) * AY + y

    halves[0:rows, :] = feats_ref[:, pl.ds(pl.multiple_of(core * half, half), quarter)]
    halves[rows : 2 * rows, :] = feats_ref[
        :, pl.ds(pl.multiple_of(core * half + quarter, quarter), quarter)
    ]
    halves[2 * rows :, :] = jnp.full((SLAB, quarter), DEAD, BF16)
    for step in range(AX):
        far = at_x(step)
        kinds = lax.broadcasted_iota(jnp.int32, (2 * rows + SLAB, BLOCK), 0)
        pick = jnp.where(kinds == idx_ref[far], 1.0, 0.0).astype(BF16)
        outgoing[rows_at(far * BLOCK, BLOCK), :] = dot_tn(pick, halves[...]).astype(BF16)
        if step == 0:
            pl.semaphore_wait(barrier, N)
        push_block(step, mine, outgoing, landed.at[core], send_sem, recv_sem)
    landed[core, own_slab, :] = outgoing[own_slab, :]

    head_of = lax.broadcasted_iota(jnp.int32, (cols, cols), 0) // DH
    head_to = lax.broadcasted_iota(jnp.int32, (cols, cols), 1) // DH
    head_mean = jnp.where(head_of == head_to, 1.0 / DH, 0.0).astype(BF16)
    which = lax.broadcasted_iota(jnp.int32, (2 * DH, rows), 0) // DH

    def part_of(b):
        return pl.ds(b * rows, rows)

    def lanes_of(pair):
        return pl.ds(pl.multiple_of(pair * 2 * DH, 2 * DH), 2 * DH)

    def normed(mixed):
        inv = lax.rsqrt(dot((mixed * mixed).astype(BF16), head_mean) + EPS)
        return mixed * inv, inv

    def consume(b, block, tile_live, first_tile):
        part = part_of(b)
        feats_t[:, part] = block.T
        unit, inv = normed(dot(block, weight_ref[1]))
        k_inv[part, :] = inv
        k_unit[part, :] = unit
        low = (unit * gain_ref[1:2, :]).astype(BF16)
        k_hat[part, :] = low
        k_hat_t[:, part] = low.T
        values[part, :] = dot(block, weight_ref[2]).astype(BF16)
        for j in range(own_tiles):
            for t in range(own_tiles):
                listed = jnp.int32(0)
                for i in range(lists_ref.shape[1]):
                    listed += jnp.where(lists_ref[t, i] == first_tile + j, 1, 0)
                mask_t[j * TILE : (j + 1) * TILE, t * TILE : (t + 1) * TILE] = (
                    tile_live(j) * listed.astype(F32)
                )

        def head_pair(pair, carry):
            lanes = lanes_of(pair)
            k_pair = k_hat[part, lanes]
            v_pair = values[part, lanes]
            for h in range(2):
                head = pair * 2 + h
                low = (jnp.exp2(dot(k_pair, q_head[head])) * mask_t[...]).astype(BF16)
                expo[head, part, :] = low
                e = low.astype(F32)
                e_dp = e * dot(v_pair, g_head[head])
                expo_dp[head, part, :] = e_dp
                if b == 0:
                    total[head] = jnp.sum(e, axis=0, keepdims=True)
                    moment[head] = jnp.sum(e_dp, axis=0, keepdims=True)
                else:
                    total[head] += jnp.sum(e, axis=0, keepdims=True)
                    moment[head] += jnp.sum(e_dp, axis=0, keepdims=True)
            return carry

        lax.fori_loop(0, heads // 2, head_pair, 0)

    own_block = feats_ref[...]
    unit, inv = normed(dot(own_block, weight_ref[0]))
    q_inv[...] = inv
    q_unit[...] = unit
    q_t[...] = (unit * (gain_ref[0:1, :] * (LOG2E / math.sqrt(DH)))).T
    g_t[...] = grad_ref[...].astype(F32).T
    for head in range(heads):
        lanes = pl.ds(head // 2 * 2 * DH, 2 * DH)
        q_head[head] = jnp.where(which == head % 2, q_t[lanes, :], 0.0).astype(BF16)
        g_head[head] = jnp.where(which == head % 2, g_t[lanes, :], 0.0).astype(BF16)
    place_in_tile = lax.broadcasted_iota(jnp.int32, (TILE, TILE), 0)
    consume(0, own_block, lambda j: jnp.where(place_in_tile < valid_ref[j], 1.0, 0.0), 0)

    for step in range(AX):
        near = lax.rem(x - step + AX, AX)
        wait_block(step, near, landed.at[core], recv_sem)
        arrived = landed.at[core, rows_at(near * BLOCK, BLOCK)]
        pair = to_other_core(arrived, arrived, core, half_send.at[step], half_recv.at[step])
        pair.wait()
        strips = []
        for plane in range(2):
            slabs = landed[plane, rows_at(near * BLOCK, BLOCK), :].astype(F32)
            slabs = slabs.reshape(AZ * AY, SLAB, quarter)
            strips.append(slabs[:, :CAP, :].reshape(BLOCK_KEYS, quarter))
            strips.append(slabs[:, CAP:, :].reshape(BLOCK_KEYS, quarter))
        mark = strips[0][:, 0:1]

        def received_live(j):
            column = jnp.broadcast_to(mark[j * TILE : (j + 1) * TILE], (TILE, TILE))
            return jnp.where(column < LIVE_MAX, 1.0, 0.0)

        block = jnp.concatenate([strip.astype(BF16) for strip in strips], axis=1)
        consume(step + 1, block, received_live, own_tiles + near * own_tiles)

    for head in range(heads):
        lanes = pl.ds(head // 2 * 2 * DH, 2 * DH)
        over = 1.0 / total[head]
        moment[head] = moment[head] * over
        total[head] = over
        q_head[head] = jnp.where(
            which == head % 2, q_t[lanes, :] * (over * (1.0 / LOG2E)), 0.0
        ).astype(BF16)
        g_head[head] = jnp.where(which == head % 2, g_t[lanes, :] * over, 0.0).astype(BF16)
    dq_t[...] = jnp.zeros(dq_t.shape, F32)

    pair_mean = head_mean[: 2 * DH, : 2 * DH]

    def norm_back(unit, inv, upstream):
        inner = dot((unit * upstream).astype(BF16), pair_mean)
        return inv * (upstream - unit * inner)

    def second_pass(pair):
        lanes = slice(pair * 2 * DH, (pair + 1) * 2 * DH)
        q_both = jnp.concatenate([q_head[pair * 2], q_head[pair * 2 + 1]], axis=1)
        g_both = jnp.concatenate([g_head[pair * 2], g_head[pair * 2 + 1]], axis=1)

        def key_block(b, carry):
            part = pl.ds(pl.multiple_of(b * rows, rows), rows)
            lows, slopes = [], []
            for head in (pair * 2, pair * 2 + 1):
                low = expo[head, part, :]
                ds = (expo_dp[head, part, :] - low.astype(F32) * moment[head]).astype(BF16)
                head_rows = slice(head * DH, (head + 1) * DH)
                dq_t[head_rows, :] += dot(k_hat_t[head_rows, part], ds)
                lows.append(low)
                slopes.append(ds)
            dv = dot_nt(jnp.concatenate(lows, axis=1), g_both)
            dk = dot_nt(jnp.concatenate(slopes, axis=1), q_both) * gain_ref[1:2, lanes]
            dk = norm_back(k_unit[part, lanes], k_inv[part, lanes], dk)
            kv_low[pair, part, 0 : 2 * DH] = dk.astype(BF16)
            kv_low[pair, part, 2 * DH :] = dv.astype(BF16)
            return carry

        lax.fori_loop(0, AX + 1, key_block, 0)
        for head in (pair * 2, pair * 2 + 1):
            head_rows = slice(head * DH, (head + 1) * DH)
            dq_t[head_rows, :] = dq_t[head_rows, :] * (total[head] * (1.0 / math.sqrt(DH)))
        upstream = dq_t[lanes, :].T * gain_ref[0:1, lanes]
        dq_low[:, lanes] = norm_back(q_unit[:, lanes], q_inv[:, lanes], upstream).astype(BF16)

    per_x = width // AX
    strip = AZ * CAP

    def gradient_columns(pair):
        lanes = slice(pair * 2 * DH, (pair + 1) * 2 * DH)
        turn = pair // 2
        for i in range(AX):
            chunk = slice(i * per_x, (i + 1) * per_x)
            both = dot(feats_t[chunk, :], kv_low[pair])
            terms = (
                dot(feats_t[chunk, 0:rows], dq_low[:, lanes]),
                both[:, : 2 * DH],
                both[:, 2 * DH :],
            )
            for c in range(3):
                term = terms[c].reshape(AZ, AY, CAP, 2 * DH)
                for j in range(AY):
                    tile = term[:, j].reshape(strip, 2 * DH).astype(BF16)
                    if pair % 2 == 0:
                        first[turn, i, c, j] = tile
                    else:
                        second[turn, j, c, i] = tile
        if pair % 2 == 0:
            return [
                axis_copy(
                    s,
                    first.at[turn, at_x(s)],
                    a_land.at[turn],
                    a_send.at[turn],
                    a_recv.at[turn],
                    peer_x(s),
                )
                for s in range(1, AX)
            ]
        return [
            axis_copy(
                s,
                second.at[turn, at_y(s)],
                b_land.at[turn],
                b_send.at[turn],
                b_recv.at[turn],
                peer_y(s),
            )
            for s in range(1, AY)
        ]

    second_pass(0)
    a_first = gradient_columns(0)
    second_pass(1)
    b_first = gradient_columns(1)
    second_pass(2)
    second_pass(3)

    pairs = []

    def term_of(step, near):
        part = part_of((step + 1) % (AX + 1))
        wanted = pl.ds(pl.multiple_of(near * half, half), half)
        dk = jnp.concatenate([kv_low[p, part, 0 : 2 * DH] for p in range(heads // 2)], axis=1)
        dv = jnp.concatenate([kv_low[p, part, 2 * DH :] for p in range(heads // 2)], axis=1)
        term = dot_nt(dk, weight_ref[1, wanted, :]) + dot_nt(dv, weight_ref[2, wanted, :])
        if step == AX:
            term += dot_nt(dq_low[...], weight_ref[0, wanted, :])
            return jnp.concatenate([term[:, :quarter], term[:, quarter:]], axis=0)
        return slabbed(term, quarter)

    def give_term(step):
        local = pl.ds(step * BLOCK, BLOCK)
        give[local, :] = term_of(step, 1 - core).astype(BF16)
        pairs.append(
            to_other_core(
                give.at[local], pair_land.at[local], core, pair_send.at[step], pair_recv.at[step]
            )
        )

    def return_term(step):
        near = lax.rem(x - step + AX, AX)
        part = rows_at(near * BLOCK, BLOCK)
        local = pl.ds(step * BLOCK, BLOCK)
        kept = term_of(step, core)
        pairs[step].wait()
        back[part, :] = (kept + pair_land[local, :].astype(F32)).astype(BF16)
        push_block((AX - step) % AX, mine, back, back_land, back_send, back_recv)

    give_term(0)
    for step in range(AX):
        give_term(step + 1)
        return_term(step)
    back_land[own_slab, :] = back[own_slab, :]
    a_second = gradient_columns(2)
    b_second = gradient_columns(3)
    keep[...] = term_of(AX, core)

    def cross_a(turn, copies):
        for copy in copies:
            copy.wait()
        a_held[turn] = total_of(first[turn, x], a_land.at[turn]).astype(BF16)
        return [
            axis_copy(
                s,
                a_held.at[turn, :, at_y(s)],
                a_land2.at[turn],
                a_send2.at[turn],
                a_recv2.at[turn],
                peer_y(s),
            )
            for s in range(1, AY)
        ]

    def cross_b(turn, copies):
        for copy in copies:
            copy.wait()
        b_held[turn] = total_of(second[turn, y], b_land.at[turn]).astype(BF16)
        return [
            axis_copy(
                s,
                b_held.at[turn, :, at_x(s)],
                b_land2.at[turn],
                b_send2.at[turn],
                b_recv2.at[turn],
                peer_x(s),
            )
            for s in range(1, AX)
        ]

    def along_z(sums, held2, landing, send_sems, recv_sems):
        sums = [part.reshape(3, AZ, CAP, 2 * DH) for part in sums]
        held2[...] = jnp.concatenate(sums, axis=2).astype(BF16)
        return [
            axis_copy(s, held2.at[:, at_z(s)], landing, send_sems, recv_sems, peer_z(s))
            for s in range(1, AZ)
        ]

    a_first = cross_a(0, a_first)
    b_first = cross_b(0, b_first)
    a_second = cross_a(1, a_second)
    b_second = cross_b(1, b_second)
    for copy in a_first + a_second:
        copy.wait()
    sums = [total_of(a_held[turn, :, y], a_land2.at[turn]) for turn in range(2)]
    a_copies = along_z(sums, a_held2, a_land3, a_send3, a_recv3)
    for copy in b_first + b_second:
        copy.wait()
    sums = [total_of(b_held[turn, :, x], b_land2.at[turn]) for turn in range(2)]
    b_copies = along_z(sums, b_held2, b_land3, b_send3, b_recv3)

    pairs[AX].wait()
    result = keep[...] + pair_land[pl.ds(AX * BLOCK, 2 * rows), :].astype(F32)
    for step in (0, 3, 2, 1):
        near = lax.rem(x - step + AX, AX)
        wait_block(step, near, back_land, back_recv)
        kinds = lax.broadcasted_iota(jnp.int32, (2 * rows, BLOCK), 0)
        pick = jnp.where(kinds == idx_ref[near], 1.0, 0.0).astype(BF16)
        result += dot(pick, back_land[rows_at(near * BLOCK, BLOCK), :])
    input_ref[:, 0:quarter] = result[:rows].astype(BF16)
    input_ref[:, quarter:] = result[rows:].astype(BF16)

    for odd, copies, held2, landing in ((0, a_copies, a_held2, a_land3), (1, b_copies, b_held2, b_land3)):
        for copy in copies:
            copy.wait()
        done = total_of(held2[:, z], landing)
        for turn in range(2):
            pair = 2 * turn + odd
            proj_ref[:, :, pair * 2 * DH : (pair + 1) * 2 * DH] = done[
                :, turn * CAP : (turn + 1) * CAP
            ]
    wait_bytes(outgoing.at[pl.ds(0, (N - 1) * SLAB)], send_sem)
    wait_bytes(back.at[pl.ds(0, (N - 1) * SLAB)], back_send)

def layer(lists, valid, idx, feats, weight, gain, grad):
    rows, width = feats.shape
    cols = grad.shape[1]
    heads = cols // DH
    keys = rows + N * CAP
    quarter = width // 4
    piece = cols // 4
    strip = AZ * CAP
    terms = N * SLAB + 2 * rows
    smem = pl.BlockSpec(memory_space=pltpu.SMEM)
    vmem = pl.BlockSpec(memory_space=pltpu.VMEM)
    ram = pltpu.VMEM
    dma = pltpu.SemaphoreType.DMA
    return pl.pallas_call(
        layer_kernel,
        out_shape=[
            jax.ShapeDtypeStruct((3, CAP, cols), F32),
            jax.ShapeDtypeStruct((rows, half_of(width)), BF16),
        ],
        in_specs=[smem, smem] + [vmem] * 5,
        out_specs=[vmem] * 2,
        scratch_shapes=[
            ram((2 * rows + SLAB, quarter), BF16),
            ram((N * SLAB, quarter), BF16),
            ram((2, N * SLAB, quarter), BF16),
            ram((width, keys), BF16),
            ram((keys, cols), BF16),
            ram((cols, keys), BF16),
            ram((keys, cols), F32),
            ram((keys, cols), F32),
            ram((keys, cols), BF16),
            ram((rows, cols), F32),
            ram((rows, cols), F32),
            ram((cols, rows), F32),
            ram((cols, rows), F32),
            ram((heads, 2 * DH, rows), BF16),
            ram((heads, 2 * DH, rows), BF16),
            ram((rows, rows), F32),
            ram((heads, keys, rows), BF16),
            ram((heads, keys, rows), F32),
            ram((heads, 1, rows), F32),
            ram((heads, 1, rows), F32),
            ram((cols, rows), F32),
            ram((heads // 2, keys, 4 * DH), BF16),
            ram((rows, cols), BF16),
            ram((2 * rows, quarter), F32),
            ram((terms, quarter), BF16),
            ram((terms, quarter), BF16),
            ram((N * SLAB, quarter), BF16),
            ram((N * SLAB, quarter), BF16),
            ram((2, AX, 3, AY, strip, piece), BF16),
            ram((2, AY, 3, AX, strip, piece), BF16),
            ram((2, AX - 1, 3, AY, strip, piece), BF16),
            ram((2, AY - 1, 3, AX, strip, piece), BF16),
            ram((2, 3, AY, strip, piece), BF16),
            ram((2, 3, AX, strip, piece), BF16),
            ram((2, AY - 1, 3, strip, piece), BF16),
            ram((2, AX - 1, 3, strip, piece), BF16),
            ram((3, AZ, 2 * CAP, piece), BF16),
            ram((3, AZ, 2 * CAP, piece), BF16),
            ram((AZ - 1, 3, 2 * CAP, piece), BF16),
            ram((AZ - 1, 3, 2 * CAP, piece), BF16),
            dma,
            dma((AX,)),
            dma((AX,)),
            dma((AX,)),
            dma((AX + 1,)),
            dma((AX + 1,)),
            dma,
            dma((AX,)),
            dma((2, AX - 1)),
            dma((2, AX - 1)),
            dma((2, AY - 1)),
            dma((2, AY - 1)),
            dma((2, AY - 1)),
            dma((2, AY - 1)),
            dma((2, AX - 1)),
            dma((2, AX - 1)),
            dma((AZ - 1,)),
            dma((AZ - 1,)),
            dma((AZ - 1,)),
            dma((AZ - 1,)),
        ],
        compiler_params=pltpu.CompilerParams(
            collective_id=0, has_side_effects=True, vmem_limit_bytes=60 * 1024 * 1024
        ),
        name="layer",
    )(lists, valid, idx, feats, weight, gain, grad)


def half_of(size):
    return size // 2


def body(
    node_feats, proj_weight, norm_gain, grad_out, tile_lists, tile_valid, send_rows, send_count
):
    rows = node_feats.shape[0]
    live = jnp.arange(CAP, dtype=jnp.int32)[None, :] < send_count.reshape(N, 1)
    left = jnp.where(live, send_rows, 2 * rows)
    right = jnp.where(live, send_rows + rows, 2 * rows)
    idx = jnp.concatenate([left, right], axis=1).reshape(AX, 1, BLOCK)
    weight = jnp.transpose(proj_weight, (1, 0, 2))
    proj_grad, input_grad = layer(
        tile_lists, tile_valid, idx, node_feats, weight, norm_gain, grad_out
    )
    return (jnp.transpose(proj_grad, (1, 0, 2)), input_grad)


def solution(mesh):
    in_specs = (
        P("dom", None),
        P(None, None, "mp"),
        P(None, "mp"),
        P("dom", "mp"),
        P("dom", None),
        P("dom"),
        P("dom", None),
        P("dom", None),
    )
    out_specs = (P("dom", None, "mp"), P("dom", "mp"))
    return jax.shard_map(body, mesh=mesh, in_specs=in_specs, out_specs=out_specs, check_vma=False)
```

```python
import math

import jax
import jax.numpy as jnp
from jax import lax
from jax.experimental import pallas as pl
from jax.experimental.pallas import tpu as pltpu
from jax.sharding import PartitionSpec as P

DH = 64
TILE = 128
CAP = 8
SLAB = 2 * CAP
EPS = 1e-06
AX, AZ, AY = 4, 8, 4
N = AX * AZ * AY
DEAD = 1024.0
LIVE_MAX = 512.0
LOG2E = math.log2(math.e)
MESH = pl.DeviceIdType.MESH
F32 = jnp.float32
BF16 = jnp.bfloat16


def dot(a, b):
    return jnp.dot(a, b, preferred_element_type=F32)


def dot_nt(a, b):
    return lax.dot_general(a, b, (((1,), (1,)), ((), ())), preferred_element_type=F32)


def dot_tn(a, b):
    return lax.dot_general(a, b, (((0,), (0,)), ((), ())), preferred_element_type=F32)


def place():
    dom = lax.axis_index("dom")
    core = lax.axis_index("mp")
    return dom, core, dom // (AZ * AY), lax.rem(dom // AY, AZ), lax.rem(dom, AY)


def rows_at(start, size):
    return pl.ds(pl.multiple_of(start, SLAB), size)


def greet_all(dom, core):
    barrier = pltpu.get_barrier_semaphore()

    def greet(i, carry):
        peer = lax.rem(dom + 1 + i, N)
        pl.semaphore_signal(barrier, inc=1, device_id={"dom": peer}, device_id_type=MESH)
        return carry

    lax.fori_loop(0, N - 1, greet, 0)
    pl.semaphore_signal(barrier, inc=1, device_id={"mp": 1 - core}, device_id_type=MESH)
    return barrier


def wait_bytes(ref, sem):
    pltpu.make_async_copy(ref, ref, sem).wait()


BLOCK = AZ * AY * SLAB
BLOCK_KEYS = AZ * AY * CAP


def push_block(step, mine, src, dst, send_sem, recv_sem):
    dom, core, x, z, y = mine
    far = lax.rem(x + step, AX)

    def push(i, carry):
        dz, dy = i // AY, lax.rem(i, AY)
        peer = far * (AZ * AY) + lax.rem(z + dz, AZ) * AY + lax.rem(y + dy, AY)
        pltpu.make_async_remote_copy(
            src_ref=src.at[rows_at(peer * SLAB, SLAB)],
            dst_ref=dst.at[rows_at(dom * SLAB, SLAB)],
            send_sem=send_sem,
            recv_sem=recv_sem.at[step],
            device_id={"dom": peer},
            device_id_type=MESH,
        ).start()
        return carry

    lax.fori_loop(1 if step == 0 else 0, AZ * AY, push, 0)


def wait_block(step, near, landed, recv_sem):
    if step == 0:
        wait_bytes(landed.at[pl.ds(0, BLOCK - SLAB)], recv_sem.at[step])
    else:
        wait_bytes(landed.at[rows_at(near * BLOCK, BLOCK)], recv_sem.at[step])


def to_other_core(src, dst, core, send_sem, recv_sem):
    copy = pltpu.make_async_remote_copy(
        src_ref=src,
        dst_ref=dst,
        send_sem=send_sem,
        recv_sem=recv_sem,
        device_id={"mp": 1 - core},
        device_id_type=MESH,
    )
    copy.start()
    return copy


def slabbed(block, width):
    count = block.shape[0] // CAP
    left = block[:, :width].reshape(count, CAP, width)
    right = block[:, width:].reshape(count, CAP, width)
    return jnp.concatenate([left, right], axis=1).reshape(count * SLAB, width)


def axis_copy(step, src, landing, send_sems, recv_sems, peer):
    copy = pltpu.make_async_remote_copy(
        src_ref=src,
        dst_ref=landing.at[step - 1],
        send_sem=send_sems.at[step - 1],
        recv_sem=recv_sems.at[step - 1],
        device_id={"dom": peer},
        device_id_type=MESH,
    )
    copy.start()
    return copy


def total_of(own_part, landing):
    result = own_part.astype(F32)
    for s in range(landing.shape[0]):
        result += landing[s].astype(F32)
    return result


def layer_kernel(
    lists_ref,
    valid_ref,
    idx_ref,
    feats_ref,
    weight_hbm,
    gain_ref,
    grad_hbm,
    proj_ref,
    input_ref,
    weight_ref,
    grad_ref,
    halves,
    outgoing,
    landed,
    feats_t,
    k_hat,
    k_hat_t,
    k_unit,
    k_inv,
    values,
    q_unit,
    q_inv,
    q_t,
    g_t,
    q_head,
    g_head,
    mask_t,
    expo,
    expo_dp,
    total,
    moment,
    dq_t,
    slope,
    kv_low,
    dq_low,
    keep,
    give,
    pair_land,
    back,
    back_land,
    first,
    second,
    a_land,
    b_land,
    a_held,
    b_held,
    a_land2,
    b_land2,
    a_held2,
    b_held2,
    a_land3,
    b_land3,
    send_sem,
    recv_sem,
    half_send,
    half_recv,
    pair_send,
    pair_recv,
    back_send,
    back_recv,
    a_send,
    a_recv,
    b_send,
    b_recv,
    a_send2,
    a_recv2,
    b_send2,
    b_recv2,
    a_send3,
    a_recv3,
    b_send3,
    b_recv3,
    load_sem,
):
    mine = place()
    dom, core, x, z, y = mine
    loads = [
        pltpu.make_async_copy(weight_hbm, weight_ref, load_sem.at[0]),
        pltpu.make_async_copy(grad_hbm, grad_ref, load_sem.at[1]),
    ]
    for load in loads:
        load.start()
    barrier = greet_all(dom, core)
    rows, width = feats_ref.shape
    cols = grad_ref.shape[1]
    half = width // 2
    quarter = half // 2
    heads = cols // DH
    own_slab = rows_at(dom * SLAB, SLAB)
    own_tiles = rows // TILE

    def at_x(step):
        return lax.rem(x + step, AX)

    def at_y(step):
        return lax.rem(y + step, AY)

    def at_z(step):
        return lax.rem(z + step, AZ)

    def peer_x(step):
        return at_x(step) * (AZ * AY) + z * AY + y

    def peer_y(step):
        return x * (AZ * AY) + z * AY + at_y(step)

    def peer_z(step):
        return x * (AZ * AY) + at_z(step) * AY + y

    halves[0:rows, :] = feats_ref[:, pl.ds(pl.multiple_of(core * half, half), quarter)]
    halves[rows : 2 * rows, :] = feats_ref[
        :, pl.ds(pl.multiple_of(core * half + quarter, quarter), quarter)
    ]
    halves[2 * rows :, :] = jnp.full((SLAB, quarter), DEAD, BF16)
    for step in range(AX):
        far = at_x(step)
        kinds = lax.broadcasted_iota(jnp.int32, (2 * rows + SLAB, BLOCK), 0)
        pick = jnp.where(kinds == idx_ref[far], 1.0, 0.0).astype(BF16)
        outgoing[rows_at(far * BLOCK, BLOCK), :] = dot_tn(pick, halves[...]).astype(BF16)
        if step == 0:
            pl.semaphore_wait(barrier, N)
        push_block(step, mine, outgoing, landed.at[core], send_sem, recv_sem)
    landed[core, own_slab, :] = outgoing[own_slab, :]

    head_of = lax.broadcasted_iota(jnp.int32, (cols, cols), 0) // DH
    head_to = lax.broadcasted_iota(jnp.int32, (cols, cols), 1) // DH
    head_mean = jnp.where(head_of == head_to, 1.0 / DH, 0.0).astype(BF16)
    which = lax.broadcasted_iota(jnp.int32, (2 * DH, rows), 0) // DH

    def part_of(b):
        return pl.ds(b * rows, rows)

    def lanes_of(pair):
        return pl.ds(pl.multiple_of(pair * 2 * DH, 2 * DH), 2 * DH)

    def normed(mixed):
        inv = lax.rsqrt(dot((mixed * mixed).astype(BF16), head_mean) + EPS)
        return mixed * inv, inv

    def consume(b, block, tile_live, first_tile):
        part = part_of(b)
        feats_t[:, part] = block.T
        unit, inv = normed(dot(block, weight_ref[1]))
        k_inv[part, :] = inv
        k_unit[part, :] = unit
        low = (unit * gain_ref[1:2, :]).astype(BF16)
        k_hat[part, :] = low
        k_hat_t[:, part] = low.T
        values[part, :] = dot(block, weight_ref[2]).astype(BF16)
        for j in range(own_tiles):
            for t in range(own_tiles):
                listed = jnp.int32(0)
                for i in range(lists_ref.shape[1]):
                    listed += jnp.where(lists_ref[t, i] == first_tile + j, 1, 0)
                mask_t[j * TILE : (j + 1) * TILE, t * TILE : (t + 1) * TILE] = (
                    tile_live(j) * listed.astype(F32)
                )

        def head_pair(pair):
            lanes = slice(pair * 2 * DH, (pair + 1) * 2 * DH)
            k_pair = k_hat[part, lanes]
            v_pair = values[part, lanes]
            for h in range(2):
                head = pair * 2 + h
                low = (jnp.exp2(dot(k_pair, q_head[head])) * mask_t[...]).astype(BF16)
                expo[head, part, :] = low
                e = low.astype(F32)
                e_dp = e * dot(v_pair, g_head[head])
                expo_dp[head, part, :] = e_dp
                if b == 0:
                    total[head] = jnp.sum(e, axis=0, keepdims=True)
                    moment[head] = jnp.sum(e_dp, axis=0, keepdims=True)
                else:
                    total[head] += jnp.sum(e, axis=0, keepdims=True)
                    moment[head] += jnp.sum(e_dp, axis=0, keepdims=True)

        for pair in range(heads // 2):
            head_pair(pair)

    for load in loads:
        load.wait()
    own_block = feats_ref[...]
    unit, inv = normed(dot(own_block, weight_ref[0]))
    q_inv[...] = inv
    q_unit[...] = unit
    q_t[...] = (unit * (gain_ref[0:1, :] * (LOG2E / math.sqrt(DH)))).T
    g_t[...] = grad_ref[...].astype(F32).T
    for head in range(heads):
        lanes = pl.ds(head // 2 * 2 * DH, 2 * DH)
        q_head[head] = jnp.where(which == head % 2, q_t[lanes, :], 0.0).astype(BF16)
        g_head[head] = jnp.where(which == head % 2, g_t[lanes, :], 0.0).astype(BF16)
    place_in_tile = lax.broadcasted_iota(jnp.int32, (TILE, TILE), 0)
    consume(0, own_block, lambda j: jnp.where(place_in_tile < valid_ref[j], 1.0, 0.0), 0)

    swaps = []
    for step in range(AX + 1):
        if step < AX:
            near = lax.rem(x - step + AX, AX)
            wait_block(step, near, landed.at[core], recv_sem)
            arrived = landed.at[core, rows_at(near * BLOCK, BLOCK)]
            swaps.append(
                to_other_core(arrived, arrived, core, half_send.at[step], half_recv.at[step])
            )
        if step == 0:
            continue
        near = lax.rem(x - (step - 1) + AX, AX)
        swaps[step - 1].wait()
        strips = []
        for plane in range(2):
            slabs = landed[plane, rows_at(near * BLOCK, BLOCK), :].astype(F32)
            slabs = slabs.reshape(AZ * AY, SLAB, quarter)
            strips.append(slabs[:, :CAP, :].reshape(BLOCK_KEYS, quarter))
            strips.append(slabs[:, CAP:, :].reshape(BLOCK_KEYS, quarter))
        mark = strips[0][:, 0:1]

        def received_live(j):
            column = jnp.broadcast_to(mark[j * TILE : (j + 1) * TILE], (TILE, TILE))
            return jnp.where(column < LIVE_MAX, 1.0, 0.0)

        block = jnp.concatenate([strip.astype(BF16) for strip in strips], axis=1)
        consume(step, block, received_live, own_tiles + near * own_tiles)

    for head in range(heads):
        lanes = pl.ds(head // 2 * 2 * DH, 2 * DH)
        over = 1.0 / total[head]
        moment[head] = moment[head] * over
        total[head] = over
        q_head[head] = jnp.where(
            which == head % 2, q_t[lanes, :] * (over * (1.0 / LOG2E)), 0.0
        ).astype(BF16)
        g_head[head] = jnp.where(which == head % 2, g_t[lanes, :] * over, 0.0).astype(BF16)

    pair_mean = head_mean[: 2 * DH, : 2 * DH]

    def norm_back(unit, inv, upstream):
        inner = dot((unit * upstream).astype(BF16), pair_mean)
        return inv * (upstream - unit * inner)

    def second_pass(pair, b):
        lanes = slice(pair * 2 * DH, (pair + 1) * 2 * DH)
        part = part_of(b)
        lows, slopes = [], []
        for h in range(2):
            head = pair * 2 + h
            low = expo[head, part, :]
            ds = expo_dp[head, part, :] - low.astype(F32) * moment[head]
            ds = ds.astype(BF16)
            slope[pair % 2, h, part, :] = ds
            lows.append(low)
            slopes.append(ds)
        g_both = jnp.concatenate([g_head[pair * 2], g_head[pair * 2 + 1]], axis=1)
        q_both = jnp.concatenate([q_head[pair * 2], q_head[pair * 2 + 1]], axis=1)
        dv = dot_nt(jnp.concatenate(lows, axis=1), g_both)
        dk = dot_nt(jnp.concatenate(slopes, axis=1), q_both) * gain_ref[1:2, lanes]
        dk = norm_back(k_unit[part, lanes], k_inv[part, lanes], dk)
        kv_low[pair, part, 0 : 2 * DH] = dk.astype(BF16)
        kv_low[pair, part, 2 * DH :] = dv.astype(BF16)

    def query_terms(pair):
        lanes = slice(pair * 2 * DH, (pair + 1) * 2 * DH)
        for h in range(2):
            head = pair * 2 + h
            head_rows = slice(head * DH, (head + 1) * DH)
            dq = dot(k_hat_t[head_rows, :], slope[pair % 2, h])
            dq_t[head_rows, :] = dq * (total[head] * (1.0 / math.sqrt(DH)))
        upstream = dq_t[lanes, :].T * gain_ref[0:1, lanes]
        dq_low[:, lanes] = norm_back(q_unit[:, lanes], q_inv[:, lanes], upstream).astype(BF16)

    per_x = width // AX
    strip = AZ * CAP

    def gradient_columns(pair):
        lanes = slice(pair * 2 * DH, (pair + 1) * 2 * DH)
        turn = pair // 2
        for i in range(AX):
            chunk = slice(i * per_x, (i + 1) * per_x)
            both = dot(feats_t[chunk, :], kv_low[pair])
            terms = (
                dot(feats_t[chunk, 0:rows], dq_low[:, lanes]),
                both[:, : 2 * DH],
                both[:, 2 * DH :],
            )
            for c in range(3):
                term = terms[c].reshape(AZ, AY, CAP, 2 * DH)
                for j in range(AY):
                    tile = term[:, j].reshape(strip, 2 * DH).astype(BF16)
                    if pair % 2 == 0:
                        first[turn, i, c, j] = tile
                    else:
                        second[turn, j, c, i] = tile
        if pair % 2 == 0:
            return [
                axis_copy(
                    s,
                    first.at[turn, at_x(s)],
                    a_land.at[turn],
                    a_send.at[turn],
                    a_recv.at[turn],
                    peer_x(s),
                )
                for s in range(1, AX)
            ]
        return [
            axis_copy(
                s,
                second.at[turn, at_y(s)],
                b_land.at[turn],
                b_send.at[turn],
                b_recv.at[turn],
                peer_y(s),
            )
            for s in range(1, AY)
        ]

    for b in range(AX + 1):
        second_pass(0, b)
    query_terms(0)
    a_first = gradient_columns(0)
    for b in range(AX + 1):
        second_pass(1, b)
    query_terms(1)
    b_first = gradient_columns(1)

    pairs = []

    def term_of(step, near):
        part = part_of((step + 1) % (AX + 1))
        wanted = pl.ds(pl.multiple_of(near * half, half), half)
        dk = jnp.concatenate([kv_low[p, part, 0 : 2 * DH] for p in range(heads // 2)], axis=1)
        dv = jnp.concatenate([kv_low[p, part, 2 * DH :] for p in range(heads // 2)], axis=1)
        term = dot_nt(dk, weight_ref[1, wanted, :]) + dot_nt(dv, weight_ref[2, wanted, :])
        if step == AX:
            term += dot_nt(dq_low[...], weight_ref[0, wanted, :])
            return jnp.concatenate([term[:, :quarter], term[:, quarter:]], axis=0)
        return slabbed(term, quarter)

    def give_term(step):
        local = pl.ds(step * BLOCK, BLOCK)
        give[local, :] = term_of(step, 1 - core).astype(BF16)
        pairs.append(
            to_other_core(
                give.at[local], pair_land.at[local], core, pair_send.at[step], pair_recv.at[step]
            )
        )

    def return_term(step):
        near = lax.rem(x - step + AX, AX)
        part = rows_at(near * BLOCK, BLOCK)
        local = pl.ds(step * BLOCK, BLOCK)
        kept = term_of(step, core)
        pairs[step].wait()
        back[part, :] = (kept + pair_land[local, :].astype(F32)).astype(BF16)
        push_block((AX - step) % AX, mine, back, back_land, back_send, back_recv)

    for step in range(AX + 1):
        second_pass(2, (step + 1) % (AX + 1))
        second_pass(3, (step + 1) % (AX + 1))
        if step == AX:
            query_terms(2)
            query_terms(3)
        give_term(step)
        if step > 0:
            return_term(step - 1)
    back_land[own_slab, :] = back[own_slab, :]
    a_second = gradient_columns(2)
    b_second = gradient_columns(3)
    keep[...] = term_of(AX, core)

    def cross_a(turn, copies):
        for copy in copies:
            copy.wait()
        a_held[turn] = total_of(first[turn, x], a_land.at[turn]).astype(BF16)
        return [
            axis_copy(
                s,
                a_held.at[turn, :, at_y(s)],
                a_land2.at[turn],
                a_send2.at[turn],
                a_recv2.at[turn],
                peer_y(s),
            )
            for s in range(1, AY)
        ]

    def cross_b(turn, copies):
        for copy in copies:
            copy.wait()
        b_held[turn] = total_of(second[turn, y], b_land.at[turn]).astype(BF16)
        return [
            axis_copy(
                s,
                b_held.at[turn, :, at_x(s)],
                b_land2.at[turn],
                b_send2.at[turn],
                b_recv2.at[turn],
                peer_x(s),
            )
            for s in range(1, AX)
        ]

    def along_z(sums, held2, landing, send_sems, recv_sems):
        sums = [part.reshape(3, AZ, CAP, 2 * DH) for part in sums]
        held2[...] = jnp.concatenate(sums, axis=2).astype(BF16)
        return [
            axis_copy(s, held2.at[:, at_z(s)], landing, send_sems, recv_sems, peer_z(s))
            for s in range(1, AZ)
        ]

    a_first = cross_a(0, a_first)
    b_first = cross_b(0, b_first)
    a_second = cross_a(1, a_second)
    b_second = cross_b(1, b_second)
    for copy in a_first + a_second:
        copy.wait()
    sums = [total_of(a_held[turn, :, y], a_land2.at[turn]) for turn in range(2)]
    a_copies = along_z(sums, a_held2, a_land3, a_send3, a_recv3)
    for copy in b_first + b_second:
        copy.wait()
    sums = [total_of(b_held[turn, :, x], b_land2.at[turn]) for turn in range(2)]
    b_copies = along_z(sums, b_held2, b_land3, b_send3, b_recv3)

    pairs[AX].wait()
    result = keep[...] + pair_land[pl.ds(AX * BLOCK, 2 * rows), :].astype(F32)
    for step in (0, 3, 2, 1):
        near = lax.rem(x - step + AX, AX)
        wait_block(step, near, back_land, back_recv)
        kinds = lax.broadcasted_iota(jnp.int32, (2 * rows, BLOCK), 0)
        pick = jnp.where(kinds == idx_ref[near], 1.0, 0.0).astype(BF16)
        result += dot(pick, back_land[rows_at(near * BLOCK, BLOCK), :])
    input_ref[:, 0:quarter] = result[:rows].astype(BF16)
    input_ref[:, quarter:] = result[rows:].astype(BF16)

    for odd, copies, held2, landing in ((0, a_copies, a_held2, a_land3), (1, b_copies, b_held2, b_land3)):
        for copy in copies:
            copy.wait()
        done = total_of(held2[:, z], landing)
        for turn in range(2):
            pair = 2 * turn + odd
            proj_ref[:, :, pair * 2 * DH : (pair + 1) * 2 * DH] = done[
                :, turn * CAP : (turn + 1) * CAP
            ]
    wait_bytes(outgoing.at[pl.ds(0, (N - 1) * SLAB)], send_sem)
    wait_bytes(back.at[pl.ds(0, (N - 1) * SLAB)], back_send)

def layer(lists, valid, idx, feats, weight, gain, grad):
    rows, width = feats.shape
    cols = grad.shape[1]
    heads = cols // DH
    keys = rows + N * CAP
    quarter = width // 4
    piece = cols // 4
    strip = AZ * CAP
    terms = N * SLAB + 2 * rows
    smem = pl.BlockSpec(memory_space=pltpu.SMEM)
    vmem = pl.BlockSpec(memory_space=pltpu.VMEM)
    hbm = pl.BlockSpec(memory_space=pl.ANY)
    ram = pltpu.VMEM
    dma = pltpu.SemaphoreType.DMA
    return pl.pallas_call(
        layer_kernel,
        out_shape=[
            jax.ShapeDtypeStruct((3, CAP, cols), F32),
            jax.ShapeDtypeStruct((rows, half_of(width)), BF16),
        ],
        in_specs=[smem, smem, vmem, vmem, hbm, vmem, hbm],
        out_specs=[vmem] * 2,
        scratch_shapes=[
            ram(weight.shape, BF16),
            ram(grad.shape, BF16),
            ram((2 * rows + SLAB, quarter), BF16),
            ram((N * SLAB, quarter), BF16),
            ram((2, N * SLAB, quarter), BF16),
            ram((width, keys), BF16),
            ram((keys, cols), BF16),
            ram((cols, keys), BF16),
            ram((keys, cols), F32),
            ram((keys, cols), F32),
            ram((keys, cols), BF16),
            ram((rows, cols), F32),
            ram((rows, cols), F32),
            ram((cols, rows), F32),
            ram((cols, rows), F32),
            ram((heads, 2 * DH, rows), BF16),
            ram((heads, 2 * DH, rows), BF16),
            ram((rows, rows), F32),
            ram((heads, keys, rows), BF16),
            ram((heads, keys, rows), F32),
            ram((heads, 1, rows), F32),
            ram((heads, 1, rows), F32),
            ram((cols, rows), F32),
            ram((2, 2, keys, rows), BF16),
            ram((heads // 2, keys, 4 * DH), BF16),
            ram((rows, cols), BF16),
            ram((2 * rows, quarter), F32),
            ram((terms, quarter), BF16),
            ram((terms, quarter), BF16),
            ram((N * SLAB, quarter), BF16),
            ram((N * SLAB, quarter), BF16),
            ram((2, AX, 3, AY, strip, piece), BF16),
            ram((2, AY, 3, AX, strip, piece), BF16),
            ram((2, AX - 1, 3, AY, strip, piece), BF16),
            ram((2, AY - 1, 3, AX, strip, piece), BF16),
            ram((2, 3, AY, strip, piece), BF16),
            ram((2, 3, AX, strip, piece), BF16),
            ram((2, AY - 1, 3, strip, piece), BF16),
            ram((2, AX - 1, 3, strip, piece), BF16),
            ram((3, AZ, 2 * CAP, piece), BF16),
            ram((3, AZ, 2 * CAP, piece), BF16),
            ram((AZ - 1, 3, 2 * CAP, piece), BF16),
            ram((AZ - 1, 3, 2 * CAP, piece), BF16),
            dma,
            dma((AX,)),
            dma((AX,)),
            dma((AX,)),
            dma((AX + 1,)),
            dma((AX + 1,)),
            dma,
            dma((AX,)),
            dma((2, AX - 1)),
            dma((2, AX - 1)),
            dma((2, AY - 1)),
            dma((2, AY - 1)),
            dma((2, AY - 1)),
            dma((2, AY - 1)),
            dma((2, AX - 1)),
            dma((2, AX - 1)),
            dma((AZ - 1,)),
            dma((AZ - 1,)),
            dma((AZ - 1,)),
            dma((AZ - 1,)),
            dma((2,)),
        ],
        compiler_params=pltpu.CompilerParams(
            collective_id=0, has_side_effects=True, vmem_limit_bytes=60 * 1024 * 1024
        ),
        name="layer",
    )(lists, valid, idx, feats, weight, gain, grad)


def half_of(size):
    return size // 2


def body(
    node_feats, proj_weight, norm_gain, grad_out, tile_lists, tile_valid, send_rows, send_count
):
    rows = node_feats.shape[0]
    live = jnp.arange(CAP, dtype=jnp.int32)[None, :] < send_count.reshape(N, 1)
    left = jnp.where(live, send_rows, 2 * rows)
    right = jnp.where(live, send_rows + rows, 2 * rows)
    idx = jnp.concatenate([left, right], axis=1).reshape(AX, 1, BLOCK)
    weight = jnp.transpose(proj_weight, (1, 0, 2))
    proj_grad, input_grad = layer(
        tile_lists, tile_valid, idx, node_feats, weight, norm_gain, grad_out
    )
    return (jnp.transpose(proj_grad, (1, 0, 2)), input_grad)


def solution(mesh):
    in_specs = (
        P("dom", None),
        P(None, None, "mp"),
        P(None, "mp"),
        P("dom", "mp"),
        P("dom", None),
        P("dom"),
        P("dom", None),
        P("dom", None),
    )
    out_specs = (P("dom", None, "mp"), P("dom", "mp"))
    return jax.shard_map(body, mesh=mesh, in_specs=in_specs, out_specs=out_specs, check_vma=False)
```

```python
import math

import jax
import jax.numpy as jnp
from jax import lax
from jax.experimental import pallas as pl
from jax.experimental.pallas import tpu as pltpu
from jax.sharding import PartitionSpec as P

DH = 64
TILE = 128
CAP = 8
SLAB = 2 * CAP
EPS = 1e-06
AX, AZ, AY = 4, 8, 4
N = AX * AZ * AY
DEAD = 1024.0
LIVE_MAX = 512.0
LOG2E = math.log2(math.e)
MESH = pl.DeviceIdType.MESH
F32 = jnp.float32
BF16 = jnp.bfloat16


def dot(a, b):
    return jnp.dot(a, b, preferred_element_type=F32)


def dot_nt(a, b):
    return lax.dot_general(a, b, (((1,), (1,)), ((), ())), preferred_element_type=F32)


def dot_tn(a, b):
    return lax.dot_general(a, b, (((0,), (0,)), ((), ())), preferred_element_type=F32)


def place():
    dom = lax.axis_index("dom")
    core = lax.axis_index("mp")
    return dom, core, dom // (AZ * AY), lax.rem(dom // AY, AZ), lax.rem(dom, AY)


def rows_at(start, size):
    return pl.ds(pl.multiple_of(start, SLAB), size)


def greet_all(dom, core):
    barrier = pltpu.get_barrier_semaphore()

    def greet(i, carry):
        peer = lax.rem(dom + 1 + i, N)
        pl.semaphore_signal(barrier, inc=1, device_id={"dom": peer}, device_id_type=MESH)
        return carry

    lax.fori_loop(0, N - 1, greet, 0)
    pl.semaphore_signal(barrier, inc=1, device_id={"mp": 1 - core}, device_id_type=MESH)
    return barrier


def wait_bytes(ref, sem):
    pltpu.make_async_copy(ref, ref, sem).wait()


BLOCK = AZ * AY * SLAB
BLOCK_KEYS = AZ * AY * CAP


def push_block(step, mine, src, dst, send_sem, recv_sem):
    dom, core, x, z, y = mine
    far = lax.rem(x + step, AX)

    def push(i, carry):
        dz, dy = i // AY, lax.rem(i, AY)
        peer = far * (AZ * AY) + lax.rem(z + dz, AZ) * AY + lax.rem(y + dy, AY)
        pltpu.make_async_remote_copy(
            src_ref=src.at[rows_at(peer * SLAB, SLAB)],
            dst_ref=dst.at[rows_at(dom * SLAB, SLAB)],
            send_sem=send_sem,
            recv_sem=recv_sem.at[step],
            device_id={"dom": peer},
            device_id_type=MESH,
        ).start()
        return carry

    lax.fori_loop(1 if step == 0 else 0, AZ * AY, push, 0)


def wait_block(step, near, landed, recv_sem):
    if step == 0:
        wait_bytes(landed.at[pl.ds(0, BLOCK - SLAB)], recv_sem.at[step])
    else:
        wait_bytes(landed.at[rows_at(near * BLOCK, BLOCK)], recv_sem.at[step])


def to_other_core(src, dst, core, send_sem, recv_sem):
    copy = pltpu.make_async_remote_copy(
        src_ref=src,
        dst_ref=dst,
        send_sem=send_sem,
        recv_sem=recv_sem,
        device_id={"mp": 1 - core},
        device_id_type=MESH,
    )
    copy.start()
    return copy


def slabbed(block, width):
    count = block.shape[0] // CAP
    left = block[:, :width].reshape(count, CAP, width)
    right = block[:, width:].reshape(count, CAP, width)
    return jnp.concatenate([left, right], axis=1).reshape(count * SLAB, width)


def axis_copy(step, src, landing, send_sems, recv_sems, peer):
    return to_peer(src, landing.at[step - 1], send_sems.at[step - 1], recv_sems.at[step - 1], peer)


def to_peer(src, dst, send_sem, recv_sem, peer):
    copy = pltpu.make_async_remote_copy(
        src_ref=src,
        dst_ref=dst,
        send_sem=send_sem,
        recv_sem=recv_sem,
        device_id={"dom": peer},
        device_id_type=MESH,
    )
    copy.start()
    return copy


PASS_UP, DONE_UP, PASS_DOWN, DONE_DOWN, LAST_UP, LAST_DOWN = range(6)


def axis_begin(blocks, at, landing, send_sems, recv_sems, peer):
    middle = blocks.shape[2] // 2
    left, right = pl.ds(0, middle), pl.ds(middle, middle)
    copies = {}
    for kind, block, side, step in (
        (PASS_UP, 2, left, 1),
        (PASS_DOWN, 2, right, 3),
        (DONE_UP, 1, right, 1),
        (DONE_DOWN, 3, left, 3),
    ):
        copies[kind] = to_peer(
            blocks.at[at(block), :, side],
            landing.at[kind],
            send_sems.at[kind],
            recv_sems.at[kind],
            peer(step),
        )
    return copies


def axis_pass(copies, blocks, at, landing, passed, send_sems, recv_sems, peer):
    middle = blocks.shape[2] // 2
    left, right = slice(0, middle), slice(middle, 2 * middle)
    for slot, arrived, kind, side, step in (
        (0, PASS_UP, LAST_UP, left, 1),
        (1, PASS_DOWN, LAST_DOWN, right, 3),
    ):
        copies[arrived].wait()
        mine = blocks[at(step), :, side].astype(F32)
        passed[slot] = (mine + landing[arrived].astype(F32)).astype(BF16)
        copies[kind] = to_peer(
            passed.at[slot], landing.at[kind], send_sems.at[kind], recv_sems.at[kind], peer(step)
        )


def axis_end(copies, own_block, landing, held):
    for kind in (DONE_UP, DONE_DOWN, LAST_UP, LAST_DOWN):
        copies[kind].wait()
    middle = own_block.shape[1] // 2
    for side, first, second in (
        (slice(0, middle), DONE_DOWN, LAST_UP),
        (slice(middle, 2 * middle), DONE_UP, LAST_DOWN),
    ):
        total = own_block[:, side].astype(F32) + landing[first].astype(F32)
        held[:, side] = (total + landing[second].astype(F32)).astype(BF16)


def total_of(own_part, landing):
    result = own_part.astype(F32)
    for s in range(landing.shape[0]):
        result += landing[s].astype(F32)
    return result


def layer_kernel(
    lists_ref,
    valid_ref,
    idx_ref,
    feats_ref,
    weight_hbm,
    gain_ref,
    grad_hbm,
    proj_ref,
    input_ref,
    weight_ref,
    grad_ref,
    halves,
    outgoing,
    landed,
    feats_t,
    k_hat,
    k_hat_t,
    k_unit,
    k_inv,
    values,
    q_unit,
    q_inv,
    q_t,
    g_t,
    q_head,
    g_head,
    mask_t,
    expo,
    expo_dp,
    total,
    moment,
    dq_t,
    slope,
    kv_low,
    dq_low,
    keep,
    give,
    pair_land,
    back,
    back_land,
    first,
    second,
    a_land,
    b_land,
    a_passed,
    b_passed,
    a_held,
    b_held,
    a_land2,
    b_land2,
    a_held2,
    b_held2,
    a_land3,
    b_land3,
    send_sem,
    recv_sem,
    half_send,
    half_recv,
    pair_send,
    pair_recv,
    back_send,
    back_recv,
    a_send,
    a_recv,
    b_send,
    b_recv,
    a_send2,
    a_recv2,
    b_send2,
    b_recv2,
    a_send3,
    a_recv3,
    b_send3,
    b_recv3,
    load_sem,
):
    mine = place()
    dom, core, x, z, y = mine
    loads = [
        pltpu.make_async_copy(weight_hbm, weight_ref, load_sem.at[0]),
        pltpu.make_async_copy(grad_hbm, grad_ref, load_sem.at[1]),
    ]
    for load in loads:
        load.start()
    barrier = greet_all(dom, core)
    rows, width = feats_ref.shape
    cols = grad_ref.shape[1]
    half = width // 2
    quarter = half // 2
    heads = cols // DH
    own_slab = rows_at(dom * SLAB, SLAB)
    own_tiles = rows // TILE

    def at_x(step):
        return lax.rem(x + step, AX)

    def at_y(step):
        return lax.rem(y + step, AY)

    def at_z(step):
        return lax.rem(z + step, AZ)

    def peer_x(step):
        return at_x(step) * (AZ * AY) + z * AY + y

    def peer_y(step):
        return x * (AZ * AY) + z * AY + at_y(step)

    def peer_z(step):
        return x * (AZ * AY) + at_z(step) * AY + y

    halves[0:rows, :] = feats_ref[:, pl.ds(pl.multiple_of(core * half, half), quarter)]
    halves[rows : 2 * rows, :] = feats_ref[
        :, pl.ds(pl.multiple_of(core * half + quarter, quarter), quarter)
    ]
    halves[2 * rows :, :] = jnp.full((SLAB, quarter), DEAD, BF16)
    for step in range(AX):
        far = at_x(step)
        kinds = lax.broadcasted_iota(jnp.int32, (2 * rows + SLAB, BLOCK), 0)
        pick = jnp.where(kinds == idx_ref[far], 1.0, 0.0).astype(BF16)
        outgoing[rows_at(far * BLOCK, BLOCK), :] = dot_tn(pick, halves[...]).astype(BF16)
        if step == 0:
            pl.semaphore_wait(barrier, N)
        push_block(step, mine, outgoing, landed.at[core], send_sem, recv_sem)
    landed[core, own_slab, :] = outgoing[own_slab, :]

    head_of = lax.broadcasted_iota(jnp.int32, (cols, cols), 0) // DH
    head_to = lax.broadcasted_iota(jnp.int32, (cols, cols), 1) // DH
    head_mean = jnp.where(head_of == head_to, 1.0 / DH, 0.0).astype(BF16)
    which = lax.broadcasted_iota(jnp.int32, (2 * DH, rows), 0) // DH

    def part_of(b):
        return pl.ds(b * rows, rows)

    def lanes_of(pair):
        return pl.ds(pl.multiple_of(pair * 2 * DH, 2 * DH), 2 * DH)

    def normed(mixed):
        inv = lax.rsqrt(dot((mixed * mixed).astype(BF16), head_mean) + EPS)
        return mixed * inv, inv

    def consume(b, block, tile_live, first_tile):
        part = part_of(b)
        feats_t[:, part] = block.T
        unit, inv = normed(dot(block, weight_ref[1]))
        k_inv[part, :] = inv
        k_unit[part, :] = unit
        low = (unit * gain_ref[1:2, :]).astype(BF16)
        k_hat[part, :] = low
        k_hat_t[:, part] = low.T
        values[part, :] = dot(block, weight_ref[2]).astype(BF16)
        for j in range(own_tiles):
            for t in range(own_tiles):
                listed = jnp.int32(0)
                for i in range(lists_ref.shape[1]):
                    listed += jnp.where(lists_ref[t, i] == first_tile + j, 1, 0)
                mask_t[j * TILE : (j + 1) * TILE, t * TILE : (t + 1) * TILE] = (
                    tile_live(j) * listed.astype(F32)
                )

        def head_pair(pair):
            lanes = slice(pair * 2 * DH, (pair + 1) * 2 * DH)
            k_pair = k_hat[part, lanes]
            v_pair = values[part, lanes]
            for h in range(2):
                head = pair * 2 + h
                low = (jnp.exp2(dot(k_pair, q_head[head])) * mask_t[...]).astype(BF16)
                expo[head, part, :] = low
                e = low.astype(F32)
                e_dp = e * dot(v_pair, g_head[head])
                expo_dp[head, part, :] = e_dp
                if b == 0:
                    total[head] = jnp.sum(e, axis=0, keepdims=True)
                    moment[head] = jnp.sum(e_dp, axis=0, keepdims=True)
                else:
                    total[head] += jnp.sum(e, axis=0, keepdims=True)
                    moment[head] += jnp.sum(e_dp, axis=0, keepdims=True)

        for pair in range(heads // 2):
            head_pair(pair)

    for load in loads:
        load.wait()
    own_block = feats_ref[...]
    unit, inv = normed(dot(own_block, weight_ref[0]))
    q_inv[...] = inv
    q_unit[...] = unit
    q_t[...] = (unit * (gain_ref[0:1, :] * (LOG2E / math.sqrt(DH)))).T
    g_t[...] = grad_ref[...].astype(F32).T
    for head in range(heads):
        lanes = pl.ds(head // 2 * 2 * DH, 2 * DH)
        q_head[head] = jnp.where(which == head % 2, q_t[lanes, :], 0.0).astype(BF16)
        g_head[head] = jnp.where(which == head % 2, g_t[lanes, :], 0.0).astype(BF16)
    place_in_tile = lax.broadcasted_iota(jnp.int32, (TILE, TILE), 0)
    consume(0, own_block, lambda j: jnp.where(place_in_tile < valid_ref[j], 1.0, 0.0), 0)

    swaps = []
    for step in range(AX + 1):
        if step < AX:
            near = lax.rem(x - step + AX, AX)
            wait_block(step, near, landed.at[core], recv_sem)
            arrived = landed.at[core, rows_at(near * BLOCK, BLOCK)]
            swaps.append(
                to_other_core(arrived, arrived, core, half_send.at[step], half_recv.at[step])
            )
        if step == 0:
            continue
        near = lax.rem(x - (step - 1) + AX, AX)
        swaps[step - 1].wait()
        strips = []
        for plane in range(2):
            slabs = landed[plane, rows_at(near * BLOCK, BLOCK), :].astype(F32)
            slabs = slabs.reshape(AZ * AY, SLAB, quarter)
            strips.append(slabs[:, :CAP, :].reshape(BLOCK_KEYS, quarter))
            strips.append(slabs[:, CAP:, :].reshape(BLOCK_KEYS, quarter))
        mark = strips[0][:, 0:1]

        def received_live(j):
            column = jnp.broadcast_to(mark[j * TILE : (j + 1) * TILE], (TILE, TILE))
            return jnp.where(column < LIVE_MAX, 1.0, 0.0)

        block = jnp.concatenate([strip.astype(BF16) for strip in strips], axis=1)
        consume(step, block, received_live, own_tiles + near * own_tiles)

    for head in range(heads):
        lanes = pl.ds(head // 2 * 2 * DH, 2 * DH)
        over = 1.0 / total[head]
        moment[head] = moment[head] * over
        total[head] = over
        q_head[head] = jnp.where(
            which == head % 2, q_t[lanes, :] * (over * (1.0 / LOG2E)), 0.0
        ).astype(BF16)
        g_head[head] = jnp.where(which == head % 2, g_t[lanes, :] * over, 0.0).astype(BF16)

    pair_mean = head_mean[: 2 * DH, : 2 * DH]

    def norm_back(unit, inv, upstream):
        inner = dot((unit * upstream).astype(BF16), pair_mean)
        return inv * (upstream - unit * inner)

    def second_pass(pair, b):
        lanes = slice(pair * 2 * DH, (pair + 1) * 2 * DH)
        part = part_of(b)
        lows, slopes = [], []
        for h in range(2):
            head = pair * 2 + h
            low = expo[head, part, :]
            ds = expo_dp[head, part, :] - low.astype(F32) * moment[head]
            ds = ds.astype(BF16)
            slope[pair % 2, h, part, :] = ds
            lows.append(low)
            slopes.append(ds)
        g_both = jnp.concatenate([g_head[pair * 2], g_head[pair * 2 + 1]], axis=1)
        q_both = jnp.concatenate([q_head[pair * 2], q_head[pair * 2 + 1]], axis=1)
        dv = dot_nt(jnp.concatenate(lows, axis=1), g_both)
        dk = dot_nt(jnp.concatenate(slopes, axis=1), q_both) * gain_ref[1:2, lanes]
        dk = norm_back(k_unit[part, lanes], k_inv[part, lanes], dk)
        kv_low[pair, part, 0 : 2 * DH] = dk.astype(BF16)
        kv_low[pair, part, 2 * DH :] = dv.astype(BF16)

    def query_terms(pair):
        lanes = slice(pair * 2 * DH, (pair + 1) * 2 * DH)
        for h in range(2):
            head = pair * 2 + h
            head_rows = slice(head * DH, (head + 1) * DH)
            dq = dot(k_hat_t[head_rows, :], slope[pair % 2, h])
            dq_t[head_rows, :] = dq * (total[head] * (1.0 / math.sqrt(DH)))
        upstream = dq_t[lanes, :].T * gain_ref[0:1, lanes]
        dq_low[:, lanes] = norm_back(q_unit[:, lanes], q_inv[:, lanes], upstream).astype(BF16)

    per_x = width // AX
    strip = AZ * CAP

    def gradient_columns(pair):
        lanes = slice(pair * 2 * DH, (pair + 1) * 2 * DH)
        turn = pair // 2
        for i in range(AX):
            chunk = slice(i * per_x, (i + 1) * per_x)
            both = dot(feats_t[chunk, :], kv_low[pair])
            terms = (
                dot(feats_t[chunk, 0:rows], dq_low[:, lanes]),
                both[:, : 2 * DH],
                both[:, 2 * DH :],
            )
            for c in range(3):
                term = terms[c].reshape(AZ, AY, CAP, 2 * DH)
                for j in range(AY):
                    tile = term[:, j].reshape(strip, 2 * DH).astype(BF16)
                    if pair % 2 == 0:
                        first[turn, i, c, j] = tile
                    else:
                        second[turn, j, c, i] = tile
        if pair % 2 == 0:
            return axis_begin(
                first.at[turn], at_x, a_land.at[turn], a_send.at[turn], a_recv.at[turn], peer_x
            )
        return axis_begin(
            second.at[turn], at_y, b_land.at[turn], b_send.at[turn], b_recv.at[turn], peer_y
        )

    def pass_a(turn, copies):
        axis_pass(
            copies,
            first.at[turn],
            at_x,
            a_land.at[turn],
            a_passed.at[turn],
            a_send.at[turn],
            a_recv.at[turn],
            peer_x,
        )

    def pass_b(turn, copies):
        axis_pass(
            copies,
            second.at[turn],
            at_y,
            b_land.at[turn],
            b_passed.at[turn],
            b_send.at[turn],
            b_recv.at[turn],
            peer_y,
        )

    for b in range(AX + 1):
        second_pass(0, b)
    query_terms(0)
    a_first = gradient_columns(0)
    for b in range(AX + 1):
        second_pass(1, b)
    query_terms(1)
    b_first = gradient_columns(1)

    pairs = []

    def term_of(step, near):
        part = part_of((step + 1) % (AX + 1))
        wanted = pl.ds(pl.multiple_of(near * half, half), half)
        dk = jnp.concatenate([kv_low[p, part, 0 : 2 * DH] for p in range(heads // 2)], axis=1)
        dv = jnp.concatenate([kv_low[p, part, 2 * DH :] for p in range(heads // 2)], axis=1)
        term = dot_nt(dk, weight_ref[1, wanted, :]) + dot_nt(dv, weight_ref[2, wanted, :])
        if step == AX:
            term += dot_nt(dq_low[...], weight_ref[0, wanted, :])
            return jnp.concatenate([term[:, :quarter], term[:, quarter:]], axis=0)
        return slabbed(term, quarter)

    def give_term(step):
        local = pl.ds(step * BLOCK, BLOCK)
        give[local, :] = term_of(step, 1 - core).astype(BF16)
        pairs.append(
            to_other_core(
                give.at[local], pair_land.at[local], core, pair_send.at[step], pair_recv.at[step]
            )
        )

    def return_term(step):
        near = lax.rem(x - step + AX, AX)
        part = rows_at(near * BLOCK, BLOCK)
        local = pl.ds(step * BLOCK, BLOCK)
        kept = term_of(step, core)
        pairs[step].wait()
        back[part, :] = (kept + pair_land[local, :].astype(F32)).astype(BF16)
        push_block((AX - step) % AX, mine, back, back_land, back_send, back_recv)

    for step in range(AX + 1):
        second_pass(2, (step + 1) % (AX + 1))
        second_pass(3, (step + 1) % (AX + 1))
        if step == AX:
            query_terms(2)
            query_terms(3)
        give_term(step)
        if step > 0:
            return_term(step - 1)
        if step == 2:
            pass_a(0, a_first)
        if step == 3:
            pass_b(0, b_first)
    back_land[own_slab, :] = back[own_slab, :]
    a_second = gradient_columns(2)
    b_second = gradient_columns(3)
    keep[...] = term_of(AX, core)

    def cross_a(turn, copies):
        axis_end(copies, first.at[turn, x], a_land.at[turn], a_held.at[turn])
        return [
            axis_copy(
                s,
                a_held.at[turn, :, at_y(s)],
                a_land2.at[turn],
                a_send2.at[turn],
                a_recv2.at[turn],
                peer_y(s),
            )
            for s in range(1, AY)
        ]

    def cross_b(turn, copies):
        axis_end(copies, second.at[turn, y], b_land.at[turn], b_held.at[turn])
        return [
            axis_copy(
                s,
                b_held.at[turn, :, at_x(s)],
                b_land2.at[turn],
                b_send2.at[turn],
                b_recv2.at[turn],
                peer_x(s),
            )
            for s in range(1, AX)
        ]

    def along_z(sums, held2, landing, send_sems, recv_sems):
        sums = [part.reshape(3, AZ, CAP, 2 * DH) for part in sums]
        held2[...] = jnp.concatenate(sums, axis=2).astype(BF16)
        return [
            axis_copy(s, held2.at[:, at_z(s)], landing, send_sems, recv_sems, peer_z(s))
            for s in range(1, AZ)
        ]

    a_first = cross_a(0, a_first)
    b_first = cross_b(0, b_first)
    pass_a(1, a_second)
    pass_b(1, b_second)
    a_second = cross_a(1, a_second)
    b_second = cross_b(1, b_second)
    for copy in a_first + a_second:
        copy.wait()
    sums = [total_of(a_held[turn, :, y], a_land2.at[turn]) for turn in range(2)]
    a_copies = along_z(sums, a_held2, a_land3, a_send3, a_recv3)
    for copy in b_first + b_second:
        copy.wait()
    sums = [total_of(b_held[turn, :, x], b_land2.at[turn]) for turn in range(2)]
    b_copies = along_z(sums, b_held2, b_land3, b_send3, b_recv3)

    pairs[AX].wait()
    result = keep[...] + pair_land[pl.ds(AX * BLOCK, 2 * rows), :].astype(F32)
    for step in (0, 3, 2, 1):
        near = lax.rem(x - step + AX, AX)
        wait_block(step, near, back_land, back_recv)
        kinds = lax.broadcasted_iota(jnp.int32, (2 * rows, BLOCK), 0)
        pick = jnp.where(kinds == idx_ref[near], 1.0, 0.0).astype(BF16)
        result += dot(pick, back_land[rows_at(near * BLOCK, BLOCK), :])
    input_ref[:, 0:quarter] = result[:rows].astype(BF16)
    input_ref[:, quarter:] = result[rows:].astype(BF16)

    for odd, copies, held2, landing in ((0, a_copies, a_held2, a_land3), (1, b_copies, b_held2, b_land3)):
        for copy in copies:
            copy.wait()
        done = total_of(held2[:, z], landing)
        for turn in range(2):
            pair = 2 * turn + odd
            proj_ref[:, :, pair * 2 * DH : (pair + 1) * 2 * DH] = done[
                :, turn * CAP : (turn + 1) * CAP
            ]
    wait_bytes(outgoing.at[pl.ds(0, (N - 1) * SLAB)], send_sem)
    wait_bytes(back.at[pl.ds(0, (N - 1) * SLAB)], back_send)

def layer(lists, valid, idx, feats, weight, gain, grad):
    rows, width = feats.shape
    cols = grad.shape[1]
    heads = cols // DH
    keys = rows + N * CAP
    quarter = width // 4
    piece = cols // 4
    strip = AZ * CAP
    terms = N * SLAB + 2 * rows
    smem = pl.BlockSpec(memory_space=pltpu.SMEM)
    vmem = pl.BlockSpec(memory_space=pltpu.VMEM)
    hbm = pl.BlockSpec(memory_space=pl.ANY)
    ram = pltpu.VMEM
    dma = pltpu.SemaphoreType.DMA
    return pl.pallas_call(
        layer_kernel,
        out_shape=[
            jax.ShapeDtypeStruct((3, CAP, cols), F32),
            jax.ShapeDtypeStruct((rows, half_of(width)), BF16),
        ],
        in_specs=[smem, smem, vmem, vmem, hbm, vmem, hbm],
        out_specs=[vmem] * 2,
        scratch_shapes=[
            ram(weight.shape, BF16),
            ram(grad.shape, BF16),
            ram((2 * rows + SLAB, quarter), BF16),
            ram((N * SLAB, quarter), BF16),
            ram((2, N * SLAB, quarter), BF16),
            ram((width, keys), BF16),
            ram((keys, cols), BF16),
            ram((cols, keys), BF16),
            ram((keys, cols), F32),
            ram((keys, cols), F32),
            ram((keys, cols), BF16),
            ram((rows, cols), F32),
            ram((rows, cols), F32),
            ram((cols, rows), F32),
            ram((cols, rows), F32),
            ram((heads, 2 * DH, rows), BF16),
            ram((heads, 2 * DH, rows), BF16),
            ram((rows, rows), F32),
            ram((heads, keys, rows), BF16),
            ram((heads, keys, rows), F32),
            ram((heads, 1, rows), F32),
            ram((heads, 1, rows), F32),
            ram((cols, rows), F32),
            ram((2, 2, keys, rows), BF16),
            ram((heads // 2, keys, 4 * DH), BF16),
            ram((rows, cols), BF16),
            ram((2 * rows, quarter), F32),
            ram((terms, quarter), BF16),
            ram((terms, quarter), BF16),
            ram((N * SLAB, quarter), BF16),
            ram((N * SLAB, quarter), BF16),
            ram((2, AX, 3, AY, strip, piece), BF16),
            ram((2, AY, 3, AX, strip, piece), BF16),
            ram((2, 6, 3, AY // 2, strip, piece), BF16),
            ram((2, 6, 3, AX // 2, strip, piece), BF16),
            ram((2, 2, 3, AY // 2, strip, piece), BF16),
            ram((2, 2, 3, AX // 2, strip, piece), BF16),
            ram((2, 3, AY, strip, piece), BF16),
            ram((2, 3, AX, strip, piece), BF16),
            ram((2, AY - 1, 3, strip, piece), BF16),
            ram((2, AX - 1, 3, strip, piece), BF16),
            ram((3, AZ, 2 * CAP, piece), BF16),
            ram((3, AZ, 2 * CAP, piece), BF16),
            ram((AZ - 1, 3, 2 * CAP, piece), BF16),
            ram((AZ - 1, 3, 2 * CAP, piece), BF16),
            dma,
            dma((AX,)),
            dma((AX,)),
            dma((AX,)),
            dma((AX + 1,)),
            dma((AX + 1,)),
            dma,
            dma((AX,)),
            dma((2, 6)),
            dma((2, 6)),
            dma((2, 6)),
            dma((2, 6)),
            dma((2, AY - 1)),
            dma((2, AY - 1)),
            dma((2, AX - 1)),
            dma((2, AX - 1)),
            dma((AZ - 1,)),
            dma((AZ - 1,)),
            dma((AZ - 1,)),
            dma((AZ - 1,)),
            dma((2,)),
        ],
        compiler_params=pltpu.CompilerParams(
            collective_id=0, has_side_effects=True, vmem_limit_bytes=60 * 1024 * 1024
        ),
        name="layer",
    )(lists, valid, idx, feats, weight, gain, grad)


def half_of(size):
    return size // 2


def body(
    node_feats, proj_weight, norm_gain, grad_out, tile_lists, tile_valid, send_rows, send_count
):
    rows = node_feats.shape[0]
    live = jnp.arange(CAP, dtype=jnp.int32)[None, :] < send_count.reshape(N, 1)
    left = jnp.where(live, send_rows, 2 * rows)
    right = jnp.where(live, send_rows + rows, 2 * rows)
    idx = jnp.concatenate([left, right], axis=1).reshape(AX, 1, BLOCK)
    weight = jnp.transpose(proj_weight, (1, 0, 2))
    proj_grad, input_grad = layer(
        tile_lists, tile_valid, idx, node_feats, weight, norm_gain, grad_out
    )
    return (jnp.transpose(proj_grad, (1, 0, 2)), input_grad)


def solution(mesh):
    in_specs = (
        P("dom", None),
        P(None, None, "mp"),
        P(None, "mp"),
        P("dom", "mp"),
        P("dom", None),
        P("dom"),
        P("dom", None),
        P("dom", None),
    )
    out_specs = (P("dom", None, "mp"), P("dom", "mp"))
    return jax.shard_map(body, mesh=mesh, in_specs=in_specs, out_specs=out_specs, check_vma=False)
```

```python
import math

import jax
import jax.numpy as jnp
from jax import lax
from jax.experimental import pallas as pl
from jax.experimental.pallas import tpu as pltpu
from jax.sharding import PartitionSpec as P

DH = 64
TILE = 128
CAP = 8
SLAB = 2 * CAP
EPS = 1e-06
AX, AZ, AY = 4, 8, 4
N = AX * AZ * AY
DEAD = 1024.0
LIVE_MAX = 512.0
LOG2E = math.log2(math.e)
MESH = pl.DeviceIdType.MESH
F32 = jnp.float32
BF16 = jnp.bfloat16


def dot(a, b):
    return jnp.dot(a, b, preferred_element_type=F32)


def dot_nt(a, b):
    return lax.dot_general(a, b, (((1,), (1,)), ((), ())), preferred_element_type=F32)


def dot_tn(a, b):
    return lax.dot_general(a, b, (((0,), (0,)), ((), ())), preferred_element_type=F32)


def place():
    dom = lax.axis_index("dom")
    core = lax.axis_index("mp")
    return dom, core, dom // (AZ * AY), lax.rem(dom // AY, AZ), lax.rem(dom, AY)


def rows_at(start, size):
    return pl.ds(pl.multiple_of(start, SLAB), size)


def greet_all(dom, core):
    barrier = pltpu.get_barrier_semaphore()

    def greet(i, carry):
        peer = lax.rem(dom + 1 + i, N)
        pl.semaphore_signal(barrier, inc=1, device_id={"dom": peer}, device_id_type=MESH)
        return carry

    lax.fori_loop(0, N - 1, greet, 0)
    pl.semaphore_signal(barrier, inc=1, device_id={"mp": 1 - core}, device_id_type=MESH)
    return barrier


def wait_bytes(ref, sem):
    pltpu.make_async_copy(ref, ref, sem).wait()


BLOCK = AZ * AY * SLAB
BLOCK_KEYS = AZ * AY * CAP


def push_block(step, mine, src, dst, send_sem, recv_sem):
    dom, core, x, z, y = mine
    far = lax.rem(x + step, AX)

    def push(i, carry):
        dz, dy = i // AY, lax.rem(i, AY)
        peer = far * (AZ * AY) + lax.rem(z + dz, AZ) * AY + lax.rem(y + dy, AY)
        pltpu.make_async_remote_copy(
            src_ref=src.at[rows_at(peer * SLAB, SLAB)],
            dst_ref=dst.at[rows_at(dom * SLAB, SLAB)],
            send_sem=send_sem,
            recv_sem=recv_sem.at[step],
            device_id={"dom": peer},
            device_id_type=MESH,
        ).start()
        return carry

    lax.fori_loop(1 if step == 0 else 0, AZ * AY, push, 0)


def wait_block(step, near, landed, recv_sem):
    if step == 0:
        wait_bytes(landed.at[pl.ds(0, BLOCK - SLAB)], recv_sem.at[step])
    else:
        wait_bytes(landed.at[rows_at(near * BLOCK, BLOCK)], recv_sem.at[step])


def to_other_core(src, dst, core, send_sem, recv_sem):
    copy = pltpu.make_async_remote_copy(
        src_ref=src,
        dst_ref=dst,
        send_sem=send_sem,
        recv_sem=recv_sem,
        device_id={"mp": 1 - core},
        device_id_type=MESH,
    )
    copy.start()
    return copy


def slabbed(block, width):
    count = block.shape[0] // CAP
    left = block[:, :width].reshape(count, CAP, width)
    right = block[:, width:].reshape(count, CAP, width)
    return jnp.concatenate([left, right], axis=1).reshape(count * SLAB, width)


def axis_copy(step, src, landing, send_sems, recv_sems, peer):
    copy = pltpu.make_async_remote_copy(
        src_ref=src,
        dst_ref=landing.at[step - 1],
        send_sem=send_sems.at[step - 1],
        recv_sem=recv_sems.at[step - 1],
        device_id={"dom": peer},
        device_id_type=MESH,
    )
    copy.start()
    return copy


def total_of(own_part, landing):
    result = own_part.astype(F32)
    for s in range(landing.shape[0]):
        result += landing[s].astype(F32)
    return result


def layer_kernel(
    lists_ref,
    valid_ref,
    idx_ref,
    feats_ref,
    weight_hbm,
    gain_ref,
    grad_hbm,
    proj_ref,
    input_ref,
    weight_ref,
    grad_ref,
    halves,
    outgoing,
    landed,
    feats_t,
    k_hat,
    k_hat_t,
    k_unit,
    k_inv,
    values,
    q_unit,
    q_inv,
    q_t,
    g_t,
    q_head,
    g_head,
    mask_t,
    expo,
    expo_dp,
    total,
    moment,
    dq_t,
    slope,
    kv_low,
    dq_low,
    keep,
    give,
    pair_land,
    back,
    back_land,
    first,
    second,
    a_land,
    b_land,
    a_held,
    b_held,
    a_land2,
    b_land2,
    a_held2,
    b_held2,
    a_land3,
    b_land3,
    send_sem,
    recv_sem,
    half_send,
    half_recv,
    pair_send,
    pair_recv,
    back_send,
    back_recv,
    a_send,
    a_recv,
    b_send,
    b_recv,
    a_send2,
    a_recv2,
    b_send2,
    b_recv2,
    a_send3,
    a_recv3,
    b_send3,
    b_recv3,
    load_sem,
):
    mine = place()
    dom, core, x, z, y = mine
    loads = [
        pltpu.make_async_copy(weight_hbm, weight_ref, load_sem.at[0]),
        pltpu.make_async_copy(grad_hbm, grad_ref, load_sem.at[1]),
    ]
    for load in loads:
        load.start()
    barrier = greet_all(dom, core)
    rows, width = feats_ref.shape
    cols = grad_ref.shape[1]
    half = width // 2
    quarter = half // 2
    heads = cols // DH
    own_slab = rows_at(dom * SLAB, SLAB)
    own_tiles = rows // TILE

    def at_x(step):
        return lax.rem(x + step, AX)

    def at_y(step):
        return lax.rem(y + step, AY)

    def at_z(step):
        return lax.rem(z + step, AZ)

    def peer_x(step):
        return at_x(step) * (AZ * AY) + z * AY + y

    def peer_y(step):
        return x * (AZ * AY) + z * AY + at_y(step)

    def peer_z(step):
        return x * (AZ * AY) + at_z(step) * AY + y

    halves[0:rows, :] = feats_ref[:, pl.ds(pl.multiple_of(core * half, half), quarter)]
    halves[rows : 2 * rows, :] = feats_ref[
        :, pl.ds(pl.multiple_of(core * half + quarter, quarter), quarter)
    ]
    halves[2 * rows :, :] = jnp.full((SLAB, quarter), DEAD, BF16)
    for step in range(AX):
        far = at_x(step)
        kinds = lax.broadcasted_iota(jnp.int32, (2 * rows + SLAB, BLOCK), 0)
        pick = jnp.where(kinds == idx_ref[far], 1.0, 0.0).astype(BF16)
        outgoing[rows_at(far * BLOCK, BLOCK), :] = dot_tn(pick, halves[...]).astype(BF16)
        if step == 0:
            pl.semaphore_wait(barrier, N)
        push_block(step, mine, outgoing, landed.at[core], send_sem, recv_sem)
    landed[core, own_slab, :] = outgoing[own_slab, :]

    head_of = lax.broadcasted_iota(jnp.int32, (cols, cols), 0) // DH
    head_to = lax.broadcasted_iota(jnp.int32, (cols, cols), 1) // DH
    head_mean = jnp.where(head_of == head_to, 1.0 / DH, 0.0).astype(BF16)
    which = lax.broadcasted_iota(jnp.int32, (2 * DH, rows), 0) // DH

    def part_of(b):
        return pl.ds(b * rows, rows)

    def lanes_of(pair):
        return pl.ds(pl.multiple_of(pair * 2 * DH, 2 * DH), 2 * DH)

    def normed(mixed):
        inv = lax.rsqrt(dot((mixed * mixed).astype(BF16), head_mean) + EPS)
        return mixed * inv, inv

    def consume(b, block, tile_live, first_tile):
        part = part_of(b)
        feats_t[:, part] = block.T
        unit, inv = normed(dot(block, weight_ref[1]))
        k_inv[part, :] = inv
        k_unit[part, :] = unit
        low = (unit * gain_ref[1:2, :]).astype(BF16)
        k_hat[part, :] = low
        k_hat_t[:, part] = low.T
        values[part, :] = dot(block, weight_ref[2]).astype(BF16)
        for j in range(own_tiles):
            for t in range(own_tiles):
                listed = jnp.int32(0)
                for i in range(lists_ref.shape[1]):
                    listed += jnp.where(lists_ref[t, i] == first_tile + j, 1, 0)
                mask_t[j * TILE : (j + 1) * TILE, t * TILE : (t + 1) * TILE] = (
                    tile_live(j) * listed.astype(F32)
                )

        def head_pair(pair):
            lanes = slice(pair * 2 * DH, (pair + 1) * 2 * DH)
            k_pair = k_hat[part, lanes]
            v_pair = values[part, lanes]
            for h in range(2):
                head = pair * 2 + h
                low = (jnp.exp2(dot(k_pair, q_head[head])) * mask_t[...]).astype(BF16)
                expo[head, part, :] = low
                e = low.astype(F32)
                e_dp = e * dot(v_pair, g_head[head])
                expo_dp[head, part, :] = e_dp
                if b == 0:
                    total[head] = jnp.sum(e, axis=0, keepdims=True)
                    moment[head] = jnp.sum(e_dp, axis=0, keepdims=True)
                else:
                    total[head] += jnp.sum(e, axis=0, keepdims=True)
                    moment[head] += jnp.sum(e_dp, axis=0, keepdims=True)

        for pair in range(heads // 2):
            head_pair(pair)

    for load in loads:
        load.wait()
    own_block = feats_ref[...]
    unit, inv = normed(dot(own_block, weight_ref[0]))
    q_inv[...] = inv
    q_unit[...] = unit
    q_t[...] = (unit * (gain_ref[0:1, :] * (LOG2E / math.sqrt(DH)))).T
    g_t[...] = grad_ref[...].astype(F32).T
    for head in range(heads):
        lanes = pl.ds(head // 2 * 2 * DH, 2 * DH)
        q_head[head] = jnp.where(which == head % 2, q_t[lanes, :], 0.0).astype(BF16)
        g_head[head] = jnp.where(which == head % 2, g_t[lanes, :], 0.0).astype(BF16)
    place_in_tile = lax.broadcasted_iota(jnp.int32, (TILE, TILE), 0)
    consume(0, own_block, lambda j: jnp.where(place_in_tile < valid_ref[j], 1.0, 0.0), 0)

    swaps = []
    for step in range(AX + 1):
        if step < AX:
            near = lax.rem(x - step + AX, AX)
            wait_block(step, near, landed.at[core], recv_sem)
            arrived = landed.at[core, rows_at(near * BLOCK, BLOCK)]
            swaps.append(
                to_other_core(arrived, arrived, core, half_send.at[step], half_recv.at[step])
            )
        if step == 0:
            continue
        near = lax.rem(x - (step - 1) + AX, AX)
        swaps[step - 1].wait()
        strips = []
        for plane in range(2):
            slabs = landed[plane, rows_at(near * BLOCK, BLOCK), :].astype(F32)
            slabs = slabs.reshape(AZ * AY, SLAB, quarter)
            strips.append(slabs[:, :CAP, :].reshape(BLOCK_KEYS, quarter))
            strips.append(slabs[:, CAP:, :].reshape(BLOCK_KEYS, quarter))
        mark = strips[0][:, 0:1]

        def received_live(j):
            column = jnp.broadcast_to(mark[j * TILE : (j + 1) * TILE], (TILE, TILE))
            return jnp.where(column < LIVE_MAX, 1.0, 0.0)

        block = jnp.concatenate([strip.astype(BF16) for strip in strips], axis=1)
        consume(step, block, received_live, own_tiles + near * own_tiles)

    for head in range(heads):
        lanes = pl.ds(head // 2 * 2 * DH, 2 * DH)
        over = 1.0 / total[head]
        moment[head] = moment[head] * over
        total[head] = over
        q_head[head] = jnp.where(
            which == head % 2, q_t[lanes, :] * (over * (1.0 / LOG2E)), 0.0
        ).astype(BF16)
        g_head[head] = jnp.where(which == head % 2, g_t[lanes, :] * over, 0.0).astype(BF16)

    pair_mean = head_mean[: 2 * DH, : 2 * DH]

    def norm_back(unit, inv, upstream):
        inner = dot((unit * upstream).astype(BF16), pair_mean)
        return inv * (upstream - unit * inner)

    def second_pass(pair, b):
        lanes = slice(pair * 2 * DH, (pair + 1) * 2 * DH)
        part = part_of(b)
        lows, slopes = [], []
        for h in range(2):
            head = pair * 2 + h
            low = expo[head, part, :]
            ds = expo_dp[head, part, :] - low.astype(F32) * moment[head]
            ds = ds.astype(BF16)
            slope[pair % 2, h, part, :] = ds
            lows.append(low)
            slopes.append(ds)
        g_both = jnp.concatenate([g_head[pair * 2], g_head[pair * 2 + 1]], axis=1)
        q_both = jnp.concatenate([q_head[pair * 2], q_head[pair * 2 + 1]], axis=1)
        dv = dot_nt(jnp.concatenate(lows, axis=1), g_both)
        dk = dot_nt(jnp.concatenate(slopes, axis=1), q_both) * gain_ref[1:2, lanes]
        dk = norm_back(k_unit[part, lanes], k_inv[part, lanes], dk)
        kv_low[pair, part, 0 : 2 * DH] = dk.astype(BF16)
        kv_low[pair, part, 2 * DH :] = dv.astype(BF16)

    def query_terms(pair):
        lanes = slice(pair * 2 * DH, (pair + 1) * 2 * DH)
        for h in range(2):
            head = pair * 2 + h
            head_rows = slice(head * DH, (head + 1) * DH)
            dq = dot(k_hat_t[head_rows, :], slope[pair % 2, h])
            dq_t[head_rows, :] = dq * (total[head] * (1.0 / math.sqrt(DH)))
        upstream = dq_t[lanes, :].T * gain_ref[0:1, lanes]
        dq_low[:, lanes] = norm_back(q_unit[:, lanes], q_inv[:, lanes], upstream).astype(BF16)

    per_x = width // AX
    strip = AZ * CAP

    def gradient_columns(pair):
        lanes = slice(pair * 2 * DH, (pair + 1) * 2 * DH)
        turn = pair // 2
        for i in range(AX):
            chunk = slice(i * per_x, (i + 1) * per_x)
            both = dot(feats_t[chunk, :], kv_low[pair])
            terms = (
                dot(feats_t[chunk, 0:rows], dq_low[:, lanes]),
                both[:, : 2 * DH],
                both[:, 2 * DH :],
            )
            for c in range(3):
                term = terms[c].reshape(AZ, AY, CAP, 2 * DH)
                for j in range(AY):
                    tile = term[:, j].reshape(strip, 2 * DH).astype(BF16)
                    if pair % 2 == 0:
                        first[turn, i, c, j] = tile
                    else:
                        second[turn, j, c, i] = tile
        if pair % 2 == 0:
            return [
                axis_copy(
                    s,
                    first.at[turn, at_x(s)],
                    a_land.at[turn],
                    a_send.at[turn],
                    a_recv.at[turn],
                    peer_x(s),
                )
                for s in range(1, AX)
            ]
        return [
            axis_copy(
                s,
                second.at[turn, at_y(s)],
                b_land.at[turn],
                b_send.at[turn],
                b_recv.at[turn],
                peer_y(s),
            )
            for s in range(1, AY)
        ]

    for b in range(AX + 1):
        second_pass(0, b)
    query_terms(0)
    a_first = gradient_columns(0)
    for b in range(AX + 1):
        second_pass(1, b)
    query_terms(1)
    b_first = gradient_columns(1)
    for b in range(AX + 1):
        second_pass(2, b)
    query_terms(2)
    a_second = gradient_columns(2)
    for b in range(AX + 1):
        second_pass(3, b)
    query_terms(3)
    b_second = gradient_columns(3)

    def cross_a(turn, copies):
        for copy in copies:
            copy.wait()
        a_held[turn] = total_of(first[turn, x], a_land.at[turn]).astype(BF16)
        return [
            axis_copy(
                s,
                a_held.at[turn, :, at_y(s)],
                a_land2.at[turn],
                a_send2.at[turn],
                a_recv2.at[turn],
                peer_y(s),
            )
            for s in range(1, AY)
        ]

    def cross_b(turn, copies):
        for copy in copies:
            copy.wait()
        b_held[turn] = total_of(second[turn, y], b_land.at[turn]).astype(BF16)
        return [
            axis_copy(
                s,
                b_held.at[turn, :, at_x(s)],
                b_land2.at[turn],
                b_send2.at[turn],
                b_recv2.at[turn],
                peer_x(s),
            )
            for s in range(1, AX)
        ]

    def along_z(sums, held2, landing, send_sems, recv_sems):
        sums = [part.reshape(3, AZ, CAP, 2 * DH) for part in sums]
        held2[...] = jnp.concatenate(sums, axis=2).astype(BF16)
        return [
            axis_copy(s, held2.at[:, at_z(s)], landing, send_sems, recv_sems, peer_z(s))
            for s in range(1, AZ)
        ]

    pairs = []

    def term_of(step, near):
        part = part_of((step + 1) % (AX + 1))
        wanted = pl.ds(pl.multiple_of(near * half, half), half)
        dk = jnp.concatenate([kv_low[p, part, 0 : 2 * DH] for p in range(heads // 2)], axis=1)
        dv = jnp.concatenate([kv_low[p, part, 2 * DH :] for p in range(heads // 2)], axis=1)
        term = dot_nt(dk, weight_ref[1, wanted, :]) + dot_nt(dv, weight_ref[2, wanted, :])
        if step == AX:
            term += dot_nt(dq_low[...], weight_ref[0, wanted, :])
            return jnp.concatenate([term[:, :quarter], term[:, quarter:]], axis=0)
        return slabbed(term, quarter)

    def give_term(step):
        local = pl.ds(step * BLOCK, BLOCK)
        give[local, :] = term_of(step, 1 - core).astype(BF16)
        pairs.append(
            to_other_core(
                give.at[local], pair_land.at[local], core, pair_send.at[step], pair_recv.at[step]
            )
        )

    def return_term(step):
        near = lax.rem(x - step + AX, AX)
        part = rows_at(near * BLOCK, BLOCK)
        local = pl.ds(step * BLOCK, BLOCK)
        kept = term_of(step, core)
        pairs[step].wait()
        back[part, :] = (kept + pair_land[local, :].astype(F32)).astype(BF16)

    def push_back(step):
        push_block((AX - step) % AX, mine, back, back_land, back_send, back_recv)

    for step in range(AX + 1):
        give_term(step)
        if step > 0:
            return_term(step - 1)
        if step > 0:
            push_back(step - 1)
        if step == 2:
            a_first = cross_a(0, a_first)
        if step == 3:
            b_first = cross_b(0, b_first)
    back_land[own_slab, :] = back[own_slab, :]
    keep[...] = term_of(AX, core)

    a_second = cross_a(1, a_second)
    b_second = cross_b(1, b_second)
    for copy in a_first + a_second:
        copy.wait()
    sums = [total_of(a_held[turn, :, y], a_land2.at[turn]) for turn in range(2)]
    a_copies = along_z(sums, a_held2, a_land3, a_send3, a_recv3)
    for copy in b_first + b_second:
        copy.wait()
    sums = [total_of(b_held[turn, :, x], b_land2.at[turn]) for turn in range(2)]
    b_copies = along_z(sums, b_held2, b_land3, b_send3, b_recv3)

    pairs[AX].wait()
    result = keep[...] + pair_land[pl.ds(AX * BLOCK, 2 * rows), :].astype(F32)
    for step in (0, 3, 2, 1):
        near = lax.rem(x - step + AX, AX)
        wait_block(step, near, back_land, back_recv)
        kinds = lax.broadcasted_iota(jnp.int32, (2 * rows, BLOCK), 0)
        pick = jnp.where(kinds == idx_ref[near], 1.0, 0.0).astype(BF16)
        result += dot(pick, back_land[rows_at(near * BLOCK, BLOCK), :])
    input_ref[:, 0:quarter] = result[:rows].astype(BF16)
    input_ref[:, quarter:] = result[rows:].astype(BF16)

    for odd, copies, held2, landing in ((0, a_copies, a_held2, a_land3), (1, b_copies, b_held2, b_land3)):
        for copy in copies:
            copy.wait()
        done = total_of(held2[:, z], landing)
        for turn in range(2):
            pair = 2 * turn + odd
            proj_ref[:, :, pair * 2 * DH : (pair + 1) * 2 * DH] = done[
                :, turn * CAP : (turn + 1) * CAP
            ]
    wait_bytes(outgoing.at[pl.ds(0, (N - 1) * SLAB)], send_sem)
    wait_bytes(back.at[pl.ds(0, (N - 1) * SLAB)], back_send)

def layer(lists, valid, idx, feats, weight, gain, grad):
    rows, width = feats.shape
    cols = grad.shape[1]
    heads = cols // DH
    keys = rows + N * CAP
    quarter = width // 4
    piece = cols // 4
    strip = AZ * CAP
    terms = N * SLAB + 2 * rows
    smem = pl.BlockSpec(memory_space=pltpu.SMEM)
    vmem = pl.BlockSpec(memory_space=pltpu.VMEM)
    hbm = pl.BlockSpec(memory_space=pl.ANY)
    ram = pltpu.VMEM
    dma = pltpu.SemaphoreType.DMA
    return pl.pallas_call(
        layer_kernel,
        out_shape=[
            jax.ShapeDtypeStruct((3, CAP, cols), F32),
            jax.ShapeDtypeStruct((rows, half_of(width)), BF16),
        ],
        in_specs=[smem, smem, vmem, vmem, hbm, vmem, hbm],
        out_specs=[vmem] * 2,
        scratch_shapes=[
            ram(weight.shape, BF16),
            ram(grad.shape, BF16),
            ram((2 * rows + SLAB, quarter), BF16),
            ram((N * SLAB, quarter), BF16),
            ram((2, N * SLAB, quarter), BF16),
            ram((width, keys), BF16),
            ram((keys, cols), BF16),
            ram((cols, keys), BF16),
            ram((keys, cols), F32),
            ram((keys, cols), F32),
            ram((keys, cols), BF16),
            ram((rows, cols), F32),
            ram((rows, cols), F32),
            ram((cols, rows), F32),
            ram((cols, rows), F32),
            ram((heads, 2 * DH, rows), BF16),
            ram((heads, 2 * DH, rows), BF16),
            ram((rows, rows), F32),
            ram((heads, keys, rows), BF16),
            ram((heads, keys, rows), F32),
            ram((heads, 1, rows), F32),
            ram((heads, 1, rows), F32),
            ram((cols, rows), F32),
            ram((2, 2, keys, rows), BF16),
            ram((heads // 2, keys, 4 * DH), BF16),
            ram((rows, cols), BF16),
            ram((2 * rows, quarter), F32),
            ram((terms, quarter), BF16),
            ram((terms, quarter), BF16),
            ram((N * SLAB, quarter), BF16),
            ram((N * SLAB, quarter), BF16),
            ram((2, AX, 3, AY, strip, piece), BF16),
            ram((2, AY, 3, AX, strip, piece), BF16),
            ram((2, AX - 1, 3, AY, strip, piece), BF16),
            ram((2, AY - 1, 3, AX, strip, piece), BF16),
            ram((2, 3, AY, strip, piece), BF16),
            ram((2, 3, AX, strip, piece), BF16),
            ram((2, AY - 1, 3, strip, piece), BF16),
            ram((2, AX - 1, 3, strip, piece), BF16),
            ram((3, AZ, 2 * CAP, piece), BF16),
            ram((3, AZ, 2 * CAP, piece), BF16),
            ram((AZ - 1, 3, 2 * CAP, piece), BF16),
            ram((AZ - 1, 3, 2 * CAP, piece), BF16),
            dma,
            dma((AX,)),
            dma((AX,)),
            dma((AX,)),
            dma((AX + 1,)),
            dma((AX + 1,)),
            dma,
            dma((AX,)),
            dma((2, AX - 1)),
            dma((2, AX - 1)),
            dma((2, AY - 1)),
            dma((2, AY - 1)),
            dma((2, AY - 1)),
            dma((2, AY - 1)),
            dma((2, AX - 1)),
            dma((2, AX - 1)),
            dma((AZ - 1,)),
            dma((AZ - 1,)),
            dma((AZ - 1,)),
            dma((AZ - 1,)),
            dma((2,)),
        ],
        compiler_params=pltpu.CompilerParams(
            collective_id=0, has_side_effects=True, vmem_limit_bytes=60 * 1024 * 1024
        ),
        name="layer",
    )(lists, valid, idx, feats, weight, gain, grad)


def half_of(size):
    return size // 2


def body(
    node_feats, proj_weight, norm_gain, grad_out, tile_lists, tile_valid, send_rows, send_count
):
    rows = node_feats.shape[0]
    live = jnp.arange(CAP, dtype=jnp.int32)[None, :] < send_count.reshape(N, 1)
    left = jnp.where(live, send_rows, 2 * rows)
    right = jnp.where(live, send_rows + rows, 2 * rows)
    idx = jnp.concatenate([left, right], axis=1).reshape(AX, 1, BLOCK)
    weight = jnp.transpose(proj_weight, (1, 0, 2))
    proj_grad, input_grad = layer(
        tile_lists, tile_valid, idx, node_feats, weight, norm_gain, grad_out
    )
    return (jnp.transpose(proj_grad, (1, 0, 2)), input_grad)


def solution(mesh):
    in_specs = (
        P("dom", None),
        P(None, None, "mp"),
        P(None, "mp"),
        P("dom", "mp"),
        P("dom", None),
        P("dom"),
        P("dom", None),
        P("dom", None),
    )
    out_specs = (P("dom", None, "mp"), P("dom", "mp"))
    return jax.shard_map(body, mesh=mesh, in_specs=in_specs, out_specs=out_specs, check_vma=False)
```

```python
import math

import jax
import jax.numpy as jnp
from jax import lax
from jax.experimental import pallas as pl
from jax.experimental.pallas import tpu as pltpu
from jax.sharding import PartitionSpec as P

DH = 64
TILE = 128
CAP = 8
SLAB = 2 * CAP
EPS = 1e-06
AX, AZ, AY = 4, 8, 4
N = AX * AZ * AY
DEAD = 1024.0
LIVE_MAX = 512.0
LOG2E = math.log2(math.e)
MESH = pl.DeviceIdType.MESH
F32 = jnp.float32
BF16 = jnp.bfloat16


def dot(a, b):
    return jnp.dot(a, b, preferred_element_type=F32)


def dot_nt(a, b):
    return lax.dot_general(a, b, (((1,), (1,)), ((), ())), preferred_element_type=F32)


def dot_tn(a, b):
    return lax.dot_general(a, b, (((0,), (0,)), ((), ())), preferred_element_type=F32)


def place():
    dom = lax.axis_index("dom")
    core = lax.axis_index("mp")
    return dom, core, dom // (AZ * AY), lax.rem(dom // AY, AZ), lax.rem(dom, AY)


def rows_at(start, size):
    return pl.ds(pl.multiple_of(start, SLAB), size)


def greet_all(dom, core):
    barrier = pltpu.get_barrier_semaphore()

    def greet(i, carry):
        peer = lax.rem(dom + 1 + i, N)
        pl.semaphore_signal(barrier, inc=1, device_id={"dom": peer}, device_id_type=MESH)
        return carry

    lax.fori_loop(0, N - 1, greet, 0)
    pl.semaphore_signal(barrier, inc=1, device_id={"mp": 1 - core}, device_id_type=MESH)
    return barrier


def wait_bytes(ref, sem):
    pltpu.make_async_copy(ref, ref, sem).wait()


BLOCK = AZ * AY * SLAB
BLOCK_KEYS = AZ * AY * CAP


def push_block(step, mine, src, dst, send_sem, recv_sem):
    dom, core, x, z, y = mine
    far = lax.rem(x + step, AX)

    def push(i, carry):
        dz, dy = i // AY, lax.rem(i, AY)
        peer = far * (AZ * AY) + lax.rem(z + dz, AZ) * AY + lax.rem(y + dy, AY)
        pltpu.make_async_remote_copy(
            src_ref=src.at[rows_at(peer * SLAB, SLAB)],
            dst_ref=dst.at[rows_at(dom * SLAB, SLAB)],
            send_sem=send_sem,
            recv_sem=recv_sem.at[step],
            device_id={"dom": peer},
            device_id_type=MESH,
        ).start()
        return carry

    lax.fori_loop(1 if step == 0 else 0, AZ * AY, push, 0)


def wait_block(step, near, landed, recv_sem):
    if step == 0:
        wait_bytes(landed.at[pl.ds(0, BLOCK - SLAB)], recv_sem.at[step])
    else:
        wait_bytes(landed.at[rows_at(near * BLOCK, BLOCK)], recv_sem.at[step])


def to_other_core(src, dst, core, send_sem, recv_sem):
    copy = pltpu.make_async_remote_copy(
        src_ref=src,
        dst_ref=dst,
        send_sem=send_sem,
        recv_sem=recv_sem,
        device_id={"mp": 1 - core},
        device_id_type=MESH,
    )
    copy.start()
    return copy


def slabbed(block, width):
    count = block.shape[0] // CAP
    left = block[:, :width].reshape(count, CAP, width)
    right = block[:, width:].reshape(count, CAP, width)
    return jnp.concatenate([left, right], axis=1).reshape(count * SLAB, width)


def axis_copy(step, src, landing, send_sems, recv_sems, peer):
    copy = pltpu.make_async_remote_copy(
        src_ref=src,
        dst_ref=landing.at[step - 1],
        send_sem=send_sems.at[step - 1],
        recv_sem=recv_sems.at[step - 1],
        device_id={"dom": peer},
        device_id_type=MESH,
    )
    copy.start()
    return copy


def total_of(own_part, landing):
    result = own_part.astype(F32)
    for s in range(landing.shape[0]):
        result += landing[s].astype(F32)
    return result


def layer_kernel(
    lists_ref,
    valid_ref,
    idx_ref,
    feats_ref,
    weight_hbm,
    gain_ref,
    grad_hbm,
    proj_ref,
    input_ref,
    weight_ref,
    grad_ref,
    halves,
    outgoing,
    landed,
    feats_t,
    k_hat,
    k_hat_t,
    k_unit,
    k_inv,
    values,
    q_unit,
    q_inv,
    q_t,
    g_t,
    q_head,
    g_head,
    mask_t,
    expo,
    expo_dp,
    total,
    moment,
    dq_t,
    slope,
    kv_low,
    dq_low,
    keep,
    give,
    pair_land,
    back,
    back_land,
    first,
    second,
    a_land,
    b_land,
    a_held,
    b_held,
    a_land2,
    b_land2,
    a_held2,
    b_held2,
    a_land3,
    b_land3,
    send_sem,
    recv_sem,
    half_send,
    half_recv,
    pair_send,
    pair_recv,
    back_send,
    back_recv,
    a_send,
    a_recv,
    b_send,
    b_recv,
    a_send2,
    a_recv2,
    b_send2,
    b_recv2,
    a_send3,
    a_recv3,
    b_send3,
    b_recv3,
    load_sem,
):
    mine = place()
    dom, core, x, z, y = mine
    loads = [
        pltpu.make_async_copy(weight_hbm, weight_ref, load_sem.at[0]),
        pltpu.make_async_copy(grad_hbm, grad_ref, load_sem.at[1]),
    ]
    for load in loads:
        load.start()
    barrier = greet_all(dom, core)
    rows, width = feats_ref.shape
    cols = grad_ref.shape[1]
    half = width // 2
    quarter = half // 2
    heads = cols // DH
    own_slab = rows_at(dom * SLAB, SLAB)
    own_tiles = rows // TILE

    def at_x(step):
        return lax.rem(x + step, AX)

    def at_y(step):
        return lax.rem(y + step, AY)

    def at_z(step):
        return lax.rem(z + step, AZ)

    def peer_x(step):
        return at_x(step) * (AZ * AY) + z * AY + y

    def peer_y(step):
        return x * (AZ * AY) + z * AY + at_y(step)

    def peer_z(step):
        return x * (AZ * AY) + at_z(step) * AY + y

    halves[0:rows, :] = feats_ref[:, pl.ds(pl.multiple_of(core * half, half), quarter)]
    halves[rows : 2 * rows, :] = feats_ref[
        :, pl.ds(pl.multiple_of(core * half + quarter, quarter), quarter)
    ]
    halves[2 * rows :, :] = jnp.full((SLAB, quarter), DEAD, BF16)
    for step in range(AX):
        far = at_x(step)
        kinds = lax.broadcasted_iota(jnp.int32, (2 * rows + SLAB, BLOCK), 0)
        pick = jnp.where(kinds == idx_ref[far], 1.0, 0.0).astype(BF16)
        outgoing[rows_at(far * BLOCK, BLOCK), :] = dot_tn(pick, halves[...]).astype(BF16)
        if step == 0:
            pl.semaphore_wait(barrier, N)
        push_block(step, mine, outgoing, landed.at[core], send_sem, recv_sem)
    landed[core, own_slab, :] = outgoing[own_slab, :]

    head_of = lax.broadcasted_iota(jnp.int32, (cols, cols), 0) // DH
    head_to = lax.broadcasted_iota(jnp.int32, (cols, cols), 1) // DH
    head_mean = jnp.where(head_of == head_to, 1.0 / DH, 0.0).astype(BF16)
    which = lax.broadcasted_iota(jnp.int32, (2 * DH, rows), 0) // DH

    def part_of(b):
        return pl.ds(b * rows, rows)

    def lanes_of(pair):
        return pl.ds(pl.multiple_of(pair * 2 * DH, 2 * DH), 2 * DH)

    def normed(mixed):
        inv = lax.rsqrt(dot((mixed * mixed).astype(BF16), head_mean) + EPS)
        return mixed * inv, inv

    def consume(b, block, tile_live, first_tile):
        part = part_of(b)
        feats_t[:, part] = block.T
        unit, inv = normed(dot(block, weight_ref[1]))
        k_inv[part, :] = inv
        k_unit[part, :] = unit
        low = (unit * gain_ref[1:2, :]).astype(BF16)
        k_hat[part, :] = low
        k_hat_t[:, part] = low.T
        values[part, :] = dot(block, weight_ref[2]).astype(BF16)
        for j in range(own_tiles):
            for t in range(own_tiles):
                listed = jnp.int32(0)
                for i in range(lists_ref.shape[1]):
                    listed += jnp.where(lists_ref[t, i] == first_tile + j, 1, 0)
                mask_t[j * TILE : (j + 1) * TILE, t * TILE : (t + 1) * TILE] = (
                    tile_live(j) * listed.astype(F32)
                )

        def head_pair(pair):
            lanes = slice(pair * 2 * DH, (pair + 1) * 2 * DH)
            k_pair = k_hat[part, lanes]
            v_pair = values[part, lanes]
            for h in range(2):
                head = pair * 2 + h
                low = (jnp.exp2(dot(k_pair, q_head[head])) * mask_t[...]).astype(BF16)
                expo[head, part, :] = low
                e = low.astype(F32)
                e_dp = e * dot(v_pair, g_head[head])
                expo_dp[head, part, :] = e_dp
                if b == 0:
                    total[head] = jnp.sum(e, axis=0, keepdims=True)
                    moment[head] = jnp.sum(e_dp, axis=0, keepdims=True)
                else:
                    total[head] += jnp.sum(e, axis=0, keepdims=True)
                    moment[head] += jnp.sum(e_dp, axis=0, keepdims=True)

        for pair in range(heads // 2):
            head_pair(pair)

    for load in loads:
        load.wait()
    own_block = feats_ref[...]
    unit, inv = normed(dot(own_block, weight_ref[0]))
    q_inv[...] = inv
    q_unit[...] = unit
    q_t[...] = (unit * (gain_ref[0:1, :] * (LOG2E / math.sqrt(DH)))).T
    g_t[...] = grad_ref[...].astype(F32).T
    for head in range(heads):
        lanes = pl.ds(head // 2 * 2 * DH, 2 * DH)
        q_head[head] = jnp.where(which == head % 2, q_t[lanes, :], 0.0).astype(BF16)
        g_head[head] = jnp.where(which == head % 2, g_t[lanes, :], 0.0).astype(BF16)
    place_in_tile = lax.broadcasted_iota(jnp.int32, (TILE, TILE), 0)
    consume(0, own_block, lambda j: jnp.where(place_in_tile < valid_ref[j], 1.0, 0.0), 0)

    swaps = []
    for step in range(AX + 1):
        if step < AX:
            near = lax.rem(x - step + AX, AX)
            wait_block(step, near, landed.at[core], recv_sem)
            arrived = landed.at[core, rows_at(near * BLOCK, BLOCK)]
            swaps.append(
                to_other_core(arrived, arrived, core, half_send.at[step], half_recv.at[step])
            )
        if step == 0:
            continue
        near = lax.rem(x - (step - 1) + AX, AX)
        swaps[step - 1].wait()
        strips = []
        for plane in range(2):
            slabs = landed[plane, rows_at(near * BLOCK, BLOCK), :].astype(F32)
            slabs = slabs.reshape(AZ * AY, SLAB, quarter)
            strips.append(slabs[:, :CAP, :].reshape(BLOCK_KEYS, quarter))
            strips.append(slabs[:, CAP:, :].reshape(BLOCK_KEYS, quarter))
        mark = strips[0][:, 0:1]

        def received_live(j):
            column = jnp.broadcast_to(mark[j * TILE : (j + 1) * TILE], (TILE, TILE))
            return jnp.where(column < LIVE_MAX, 1.0, 0.0)

        block = jnp.concatenate([strip.astype(BF16) for strip in strips], axis=1)
        consume(step, block, received_live, own_tiles + near * own_tiles)

    for head in range(heads):
        lanes = pl.ds(head // 2 * 2 * DH, 2 * DH)
        over = 1.0 / total[head]
        moment[head] = moment[head] * over
        total[head] = over
        q_head[head] = jnp.where(
            which == head % 2, q_t[lanes, :] * (over * (1.0 / LOG2E)), 0.0
        ).astype(BF16)
        g_head[head] = jnp.where(which == head % 2, g_t[lanes, :] * over, 0.0).astype(BF16)

    pair_mean = head_mean[: 2 * DH, : 2 * DH]

    def norm_back(unit, inv, upstream):
        inner = dot((unit * upstream).astype(BF16), pair_mean)
        return inv * (upstream - unit * inner)

    def second_pass(pair, b):
        lanes = slice(pair * 2 * DH, (pair + 1) * 2 * DH)
        part = part_of(b)
        lows, slopes = [], []
        for h in range(2):
            head = pair * 2 + h
            low = expo[head, part, :]
            ds = expo_dp[head, part, :] - low.astype(F32) * moment[head]
            ds = ds.astype(BF16)
            slope[pair % 2, h, part, :] = ds
            lows.append(low)
            slopes.append(ds)
        g_both = jnp.concatenate([g_head[pair * 2], g_head[pair * 2 + 1]], axis=1)
        q_both = jnp.concatenate([q_head[pair * 2], q_head[pair * 2 + 1]], axis=1)
        dv = dot_nt(jnp.concatenate(lows, axis=1), g_both)
        dk = dot_nt(jnp.concatenate(slopes, axis=1), q_both) * gain_ref[1:2, lanes]
        dk = norm_back(k_unit[part, lanes], k_inv[part, lanes], dk)
        kv_low[pair, part, 0 : 2 * DH] = dk.astype(BF16)
        kv_low[pair, part, 2 * DH :] = dv.astype(BF16)

    def query_terms(pair):
        lanes = slice(pair * 2 * DH, (pair + 1) * 2 * DH)
        for h in range(2):
            head = pair * 2 + h
            head_rows = slice(head * DH, (head + 1) * DH)
            dq = dot(k_hat_t[head_rows, :], slope[pair % 2, h])
            dq_t[head_rows, :] = dq * (total[head] * (1.0 / math.sqrt(DH)))
        upstream = dq_t[lanes, :].T * gain_ref[0:1, lanes]
        dq_low[:, lanes] = norm_back(q_unit[:, lanes], q_inv[:, lanes], upstream).astype(BF16)

    per_x = width // AX
    strip = AZ * CAP

    def gradient_columns(pair):
        lanes = slice(pair * 2 * DH, (pair + 1) * 2 * DH)
        turn = pair // 2
        for i in range(AX):
            chunk = slice(i * per_x, (i + 1) * per_x)
            both = dot(feats_t[chunk, :], kv_low[pair])
            terms = (
                dot(feats_t[chunk, 0:rows], dq_low[:, lanes]),
                both[:, : 2 * DH],
                both[:, 2 * DH :],
            )
            for c in range(3):
                term = terms[c].reshape(AZ, AY, CAP, 2 * DH)
                for j in range(AY):
                    tile = term[:, j].reshape(strip, 2 * DH).astype(BF16)
                    if pair % 2 == 0:
                        first[turn, i, c, j] = tile
                    else:
                        second[turn, j, c, i] = tile
        if pair % 2 == 0:
            return [
                axis_copy(
                    s,
                    first.at[turn, at_x(s)],
                    a_land.at[turn],
                    a_send.at[turn],
                    a_recv.at[turn],
                    peer_x(s),
                )
                for s in range(1, AX)
            ]
        return [
            axis_copy(
                s,
                second.at[turn, at_y(s)],
                b_land.at[turn],
                b_send.at[turn],
                b_recv.at[turn],
                peer_y(s),
            )
            for s in range(1, AY)
        ]

    for b in range(AX + 1):
        second_pass(0, b)
    query_terms(0)
    a_first = gradient_columns(0)
    for b in range(AX + 1):
        second_pass(1, b)
    query_terms(1)
    b_first = gradient_columns(1)
    for b in range(AX + 1):
        second_pass(2, b)
    query_terms(2)
    a_second = gradient_columns(2)
    for b in range(AX + 1):
        second_pass(3, b)
    query_terms(3)

    def cross_a(turn, copies):
        for copy in copies:
            copy.wait()
        a_held[turn] = total_of(first[turn, x], a_land.at[turn]).astype(BF16)
        return [
            axis_copy(
                s,
                a_held.at[turn, :, at_y(s)],
                a_land2.at[turn],
                a_send2.at[turn],
                a_recv2.at[turn],
                peer_y(s),
            )
            for s in range(1, AY)
        ]

    def cross_b(turn, copies):
        for copy in copies:
            copy.wait()
        b_held[turn] = total_of(second[turn, y], b_land.at[turn]).astype(BF16)
        return [
            axis_copy(
                s,
                b_held.at[turn, :, at_x(s)],
                b_land2.at[turn],
                b_send2.at[turn],
                b_recv2.at[turn],
                peer_x(s),
            )
            for s in range(1, AX)
        ]

    def along_z(sums, held2, landing, send_sems, recv_sems):
        sums = [part.reshape(3, AZ, CAP, 2 * DH) for part in sums]
        held2[...] = jnp.concatenate(sums, axis=2).astype(BF16)
        return [
            axis_copy(s, held2.at[:, at_z(s)], landing, send_sems, recv_sems, peer_z(s))
            for s in range(1, AZ)
        ]

    pairs = []

    def term_of(step, near):
        part = part_of((step + 1) % (AX + 1))
        wanted = pl.ds(pl.multiple_of(near * half, half), half)
        dk = jnp.concatenate([kv_low[p, part, 0 : 2 * DH] for p in range(heads // 2)], axis=1)
        dv = jnp.concatenate([kv_low[p, part, 2 * DH :] for p in range(heads // 2)], axis=1)
        term = dot_nt(dk, weight_ref[1, wanted, :]) + dot_nt(dv, weight_ref[2, wanted, :])
        if step == AX:
            term += dot_nt(dq_low[...], weight_ref[0, wanted, :])
            return jnp.concatenate([term[:, :quarter], term[:, quarter:]], axis=0)
        return slabbed(term, quarter)

    def give_term(step):
        local = pl.ds(step * BLOCK, BLOCK)
        give[local, :] = term_of(step, 1 - core).astype(BF16)
        pairs.append(
            to_other_core(
                give.at[local], pair_land.at[local], core, pair_send.at[step], pair_recv.at[step]
            )
        )

    def return_term(step):
        near = lax.rem(x - step + AX, AX)
        part = rows_at(near * BLOCK, BLOCK)
        local = pl.ds(step * BLOCK, BLOCK)
        kept = term_of(step, core)
        pairs[step].wait()
        back[part, :] = (kept + pair_land[local, :].astype(F32)).astype(BF16)

    def push_back(step):
        push_block((AX - step) % AX, mine, back, back_land, back_send, back_recv)

    for step in range(AX + 1):
        give_term(step)
        if step == 1:
            b_second = gradient_columns(3)
        if step > 0:
            return_term(step - 1)
        if step > 0:
            push_back(step - 1)
        if step == 2:
            a_first = cross_a(0, a_first)
        if step == 3:
            b_first = cross_b(0, b_first)
    back_land[own_slab, :] = back[own_slab, :]
    keep[...] = term_of(AX, core)

    a_second = cross_a(1, a_second)
    b_second = cross_b(1, b_second)
    for copy in a_first + a_second:
        copy.wait()
    sums = [total_of(a_held[turn, :, y], a_land2.at[turn]) for turn in range(2)]
    a_copies = along_z(sums, a_held2, a_land3, a_send3, a_recv3)
    for copy in b_first + b_second:
        copy.wait()
    sums = [total_of(b_held[turn, :, x], b_land2.at[turn]) for turn in range(2)]
    b_copies = along_z(sums, b_held2, b_land3, b_send3, b_recv3)

    pairs[AX].wait()
    result = keep[...] + pair_land[pl.ds(AX * BLOCK, 2 * rows), :].astype(F32)
    for step in (0, 3, 2, 1):
        near = lax.rem(x - step + AX, AX)
        wait_block(step, near, back_land, back_recv)
        kinds = lax.broadcasted_iota(jnp.int32, (2 * rows, BLOCK), 0)
        pick = jnp.where(kinds == idx_ref[near], 1.0, 0.0).astype(BF16)
        result += dot(pick, back_land[rows_at(near * BLOCK, BLOCK), :])
    input_ref[:, 0:quarter] = result[:rows].astype(BF16)
    input_ref[:, quarter:] = result[rows:].astype(BF16)

    for odd, copies, held2, landing in ((0, a_copies, a_held2, a_land3), (1, b_copies, b_held2, b_land3)):
        for copy in copies:
            copy.wait()
        done = total_of(held2[:, z], landing)
        for turn in range(2):
            pair = 2 * turn + odd
            proj_ref[:, :, pair * 2 * DH : (pair + 1) * 2 * DH] = done[
                :, turn * CAP : (turn + 1) * CAP
            ]
    wait_bytes(outgoing.at[pl.ds(0, (N - 1) * SLAB)], send_sem)
    wait_bytes(back.at[pl.ds(0, (N - 1) * SLAB)], back_send)

def layer(lists, valid, idx, feats, weight, gain, grad):
    rows, width = feats.shape
    cols = grad.shape[1]
    heads = cols // DH
    keys = rows + N * CAP
    quarter = width // 4
    piece = cols // 4
    strip = AZ * CAP
    terms = N * SLAB + 2 * rows
    smem = pl.BlockSpec(memory_space=pltpu.SMEM)
    vmem = pl.BlockSpec(memory_space=pltpu.VMEM)
    hbm = pl.BlockSpec(memory_space=pl.ANY)
    ram = pltpu.VMEM
    dma = pltpu.SemaphoreType.DMA
    return pl.pallas_call(
        layer_kernel,
        out_shape=[
            jax.ShapeDtypeStruct((3, CAP, cols), F32),
            jax.ShapeDtypeStruct((rows, half_of(width)), BF16),
        ],
        in_specs=[smem, smem, vmem, vmem, hbm, vmem, hbm],
        out_specs=[vmem] * 2,
        scratch_shapes=[
            ram(weight.shape, BF16),
            ram(grad.shape, BF16),
            ram((2 * rows + SLAB, quarter), BF16),
            ram((N * SLAB, quarter), BF16),
            ram((2, N * SLAB, quarter), BF16),
            ram((width, keys), BF16),
            ram((keys, cols), BF16),
            ram((cols, keys), BF16),
            ram((keys, cols), F32),
            ram((keys, cols), F32),
            ram((keys, cols), BF16),
            ram((rows, cols), F32),
            ram((rows, cols), F32),
            ram((cols, rows), F32),
            ram((cols, rows), F32),
            ram((heads, 2 * DH, rows), BF16),
            ram((heads, 2 * DH, rows), BF16),
            ram((rows, rows), F32),
            ram((heads, keys, rows), BF16),
            ram((heads, keys, rows), F32),
            ram((heads, 1, rows), F32),
            ram((heads, 1, rows), F32),
            ram((cols, rows), F32),
            ram((2, 2, keys, rows), BF16),
            ram((heads // 2, keys, 4 * DH), BF16),
            ram((rows, cols), BF16),
            ram((2 * rows, quarter), F32),
            ram((terms, quarter), BF16),
            ram((terms, quarter), BF16),
            ram((N * SLAB, quarter), BF16),
            ram((N * SLAB, quarter), BF16),
            ram((2, AX, 3, AY, strip, piece), BF16),
            ram((2, AY, 3, AX, strip, piece), BF16),
            ram((2, AX - 1, 3, AY, strip, piece), BF16),
            ram((2, AY - 1, 3, AX, strip, piece), BF16),
            ram((2, 3, AY, strip, piece), BF16),
            ram((2, 3, AX, strip, piece), BF16),
            ram((2, AY - 1, 3, strip, piece), BF16),
            ram((2, AX - 1, 3, strip, piece), BF16),
            ram((3, AZ, 2 * CAP, piece), BF16),
            ram((3, AZ, 2 * CAP, piece), BF16),
            ram((AZ - 1, 3, 2 * CAP, piece), BF16),
            ram((AZ - 1, 3, 2 * CAP, piece), BF16),
            dma,
            dma((AX,)),
            dma((AX,)),
            dma((AX,)),
            dma((AX + 1,)),
            dma((AX + 1,)),
            dma,
            dma((AX,)),
            dma((2, AX - 1)),
            dma((2, AX - 1)),
            dma((2, AY - 1)),
            dma((2, AY - 1)),
            dma((2, AY - 1)),
            dma((2, AY - 1)),
            dma((2, AX - 1)),
            dma((2, AX - 1)),
            dma((AZ - 1,)),
            dma((AZ - 1,)),
            dma((AZ - 1,)),
            dma((AZ - 1,)),
            dma((2,)),
        ],
        compiler_params=pltpu.CompilerParams(
            collective_id=0, has_side_effects=True, vmem_limit_bytes=60 * 1024 * 1024
        ),
        name="layer",
    )(lists, valid, idx, feats, weight, gain, grad)


def half_of(size):
    return size // 2


def body(
    node_feats, proj_weight, norm_gain, grad_out, tile_lists, tile_valid, send_rows, send_count
):
    rows = node_feats.shape[0]
    live = jnp.arange(CAP, dtype=jnp.int32)[None, :] < send_count.reshape(N, 1)
    left = jnp.where(live, send_rows, 2 * rows)
    right = jnp.where(live, send_rows + rows, 2 * rows)
    idx = jnp.concatenate([left, right], axis=1).reshape(AX, 1, BLOCK)
    weight = jnp.transpose(proj_weight, (1, 0, 2))
    proj_grad, input_grad = layer(
        tile_lists, tile_valid, idx, node_feats, weight, norm_gain, grad_out
    )
    return (jnp.transpose(proj_grad, (1, 0, 2)), input_grad)


def solution(mesh):
    in_specs = (
        P("dom", None),
        P(None, None, "mp"),
        P(None, "mp"),
        P("dom", "mp"),
        P("dom", None),
        P("dom"),
        P("dom", None),
        P("dom", None),
    )
    out_specs = (P("dom", None, "mp"), P("dom", "mp"))
    return jax.shard_map(body, mesh=mesh, in_specs=in_specs, out_specs=out_specs, check_vma=False)
```
